32 devices in a mesh: tm: 16 (over z, y, core), head: 2 (over x).
Axes of the slice: x: 2, y: 2, z: 4, core: 2. Of those that a mesh axis runs over, the one named last changes fastest.
Arguments:
- queries: bfloat16 [4096, 2048], P('tm', 'head'), may hold values from -48 to 48
- keys: bfloat16 [4096, 2048], P('tm', 'head'), may hold values from -6 to 6
- values_in: bfloat16 [4096, 2048], P('tm', 'head'), may hold values from -32 to 32
- teacher: bfloat16 [4096, 2048], P('tm', 'head'), may hold values from -6 to 6
- gain: float32 [2048], P('head'), may hold values from 0.25 to 1.75
- conv_weight: float32 [4, 2048], P(None, 'head'), may hold values from -3 to 3
- block_bits: int32 [32, 6], P('tm'), may hold values from 0 to 1, as said below
- mask_pos: int32 [32, 64], P('tm'), may hold values from 0 to 127, as said below
Outputs:
- query_grad: bfloat16 [4096, 2048], P('tm', 'head')
- key_grad: bfloat16 [4096, 2048], P('tm', 'head')
- value_grad: bfloat16 [4096, 2048], P('tm', 'head')
- conv_grad: float32 [4, 2048], P(None, 'head')
The draws below stay inside these ranges and needn't reach their ends.
Inputs may be any that keep to these rules, and one draw needn't show every extreme that they name: `block_bits`: column 0 of every row is 1. `mask_pos`: each row names 64 different positions.
All inputs are finite; a program needn't handle non-finite values.
Results may differ from the reference program's by a relative error of at most 0.0095.
Values may be sent and summed in bfloat16 or wider, within the bound.
A program may use at most 64 MiB of HBM per device.

```python
import jax
import jax.numpy as jnp
from jax import lax

D = 2048
HEADS = 16
HD = 128
TOK_DEV = 256
BLK = 128
KW = 4
MPB = 64
REACH = 3
TOKENS = 4096
NBLK = 32
WIN = 6
N_TM = 16


def query_key_pair(key):
    base_query = jax.random.fold_in(key, 101)
    base_key = jax.random.fold_in(key, 202)
    query_all = jnp.clip(jax.random.normal(base_query, (TOKENS, D), jnp.float32), -6.0, 6.0)
    key_all = jnp.clip(jax.random.normal(base_key, (TOKENS, D), jnp.float32), -6.0, 6.0)
    return (query_all, key_all)


def draw_queries(key, part):
    return query_key_pair(key)[0].astype(jnp.bfloat16)


def draw_keys(key, part):
    return query_key_pair(key)[1].astype(jnp.bfloat16)


def draw_values_in(key, part):
    channel = jnp.arange(D, dtype=jnp.float32)
    channel_scale = 0.6 * 3.0 ** (channel / (D - 1))
    drawn = jnp.clip(jax.random.normal(jax.random.fold_in(key, 7), (TOKENS, D), jnp.float32), -6.0, 6.0) * channel_scale[None, :]
    return drawn.astype(jnp.bfloat16)


def draw_block_bits(key, part):
    device_count = TOKENS // TOK_DEV
    density_level = jax.random.randint(jax.random.fold_in(key, 1), (device_count,), 0, 8)
    row_level = jnp.repeat(density_level, TOK_DEV // BLK)
    random_draws = jax.random.randint(jax.random.fold_in(key, 2), (NBLK, WIN), 0, 8)
    block_flags = (random_draws <= row_level[:, None]).astype(jnp.int32)
    column = jnp.arange(WIN, dtype=jnp.int32)
    return jnp.where(column[None, :] == 0, 1, block_flags).astype(jnp.int32)


def draw_mask_pos(key, part):
    key_list = jax.random.split(key, NBLK)

    def one_block(sub_key):
        return jax.random.permutation(sub_key, BLK)[:MPB]
    return jax.vmap(one_block)(key_list).astype(jnp.int32)


def shard_levels(key, shape, cuts, least, largest):
    def one(dim, shards_of):
        steps = jax.random.uniform(jax.random.fold_in(jax.random.fold_in(key, 6), dim), (shards_of,), jnp.float32, least / len(cuts), largest / len(cuts))
        return jnp.repeat(jnp.exp(steps), shape[dim] // shards_of).reshape((-1,) + (1,) * (len(shape) - dim - 1))

    factor_of = one(*cuts[0])
    for cut in cuts[1:]:
        factor_of = factor_of * one(*cut)
    return factor_of


def noise(own_key, dims, spread, reach, cuts=(), kind=jnp.bfloat16):
    values = spread * jax.random.normal(own_key, dims, jnp.float32)
    if cuts:
        values = values * shard_levels(own_key, dims, cuts, -0.22, 0.18)
    return jnp.clip(values, -reach, reach).astype(kind)


def setup_inputs(seed: int = 0) -> dict:
    arg_keys = jax.random.split(jax.random.key(seed), 9)
    queries = draw_queries(jax.random.fold_in(arg_keys[8], 71), 0)
    keys = draw_keys(jax.random.fold_in(arg_keys[8], 71), 0)
    values_in = draw_values_in(jax.random.fold_in(arg_keys[8], 71), 0)
    teacher = noise(arg_keys[3], (TOKENS, D), 1.0, 6.0, ((0, 16), (1, 2)))
    gain = jnp.clip(1.0 + 0.15 * jax.random.normal(arg_keys[4], (D,), jnp.float32), 0.25, 1.75)
    conv_weight = noise(arg_keys[5], (KW, D), 0.5, 3.0, ((1, 2),), jnp.float32)
    block_bits = draw_block_bits(jax.random.fold_in(arg_keys[8], 71), 0)
    mask_pos = draw_mask_pos(jax.random.fold_in(arg_keys[8], 71), 0)
    return dict(queries=queries, keys=keys, values_in=values_in, teacher=teacher, gain=gain, conv_weight=conv_weight, block_bits=block_bits, mask_pos=mask_pos)


NEG_FILL = -1e+30
NORM_EPS = 1e-06

def split_heads(array):
    return array.reshape(array.shape[0], HEADS, HD)

def device_rows(array, device):
    return lax.dynamic_slice_in_dim(array, jnp.clip(device, 0, N_TM - 1) * TOK_DEV, TOK_DEV, 0)

def pair_mask(block_bits, qdevice, kdevice):
    qpos = qdevice * TOK_DEV + jnp.arange(TOK_DEV, dtype=jnp.int32)
    kpos = kdevice * TOK_DEV + jnp.arange(TOK_DEV, dtype=jnp.int32)
    relative = qpos[:, None] // BLK - kpos[None, :] // BLK
    bit_rows = lax.dynamic_slice_in_dim(block_bits, jnp.clip(qdevice, 0, N_TM - 1) * (TOK_DEV // BLK), TOK_DEV // BLK, 0)
    bit_rows = jnp.repeat(bit_rows, BLK, axis=0)
    picked = jnp.take_along_axis(bit_rows, jnp.clip(relative, 0, WIN - 1).astype(jnp.int32), axis=1)
    return (kdevice >= 0) & (qdevice < N_TM) & (kpos[None, :] <= qpos[:, None]) & (relative < WIN) & (picked > 0)

def reference(queries, keys, values_in, teacher, gain, conv_weight, block_bits, mask_pos):
    score_scale = HD ** (-0.5)
    padded_in = jnp.concatenate([jnp.zeros((KW - 1, D), jnp.float32), values_in.astype(jnp.float32)], 0)
    conv_sum = jnp.zeros((TOKENS, D), jnp.float32)
    for tap_index in range(KW):
        conv_sum = conv_sum + conv_weight[tap_index] * padded_in[KW - 1 - tap_index:KW - 1 - tap_index + TOKENS]
    values = conv_sum.astype(jnp.bfloat16)
    query_f = queries.astype(jnp.float32)
    key_f = keys.astype(jnp.float32)
    value_f = values.astype(jnp.float32)

    def pair_scores(qdevice, kdevice):
        raw_scores = jnp.einsum('thd,uhd->htu', split_heads(device_rows(query_f, qdevice)), split_heads(device_rows(key_f, kdevice))) * score_scale
        allowed = pair_mask(block_bits, qdevice, kdevice)
        return (jnp.where(allowed[None], raw_scores, NEG_FILL), allowed)

    def forward_block(qdevice):
        pairs = [pair_scores(qdevice, qdevice - distance) for distance in range(REACH + 1)]
        row_peak = lax.optimization_barrier(jnp.max(pairs[0][0], axis=2))
        for distance in range(1, REACH + 1):
            row_peak = jnp.maximum(row_peak, lax.optimization_barrier(jnp.max(pairs[distance][0], axis=2)))
        expos = [jnp.where(allowed[None], jnp.exp(scores - row_peak[..., None]), 0.0) for scores, allowed in pairs]
        row_total = jnp.zeros_like(row_peak)
        for distance in range(REACH + 1):
            row_total = row_total + lax.optimization_barrier(jnp.sum(expos[distance], axis=2))
        attended = jnp.zeros((TOK_DEV, HEADS, HD), jnp.float32)
        for distance in range(REACH + 1):
            weights = (expos[distance] / row_total[..., None]).astype(jnp.bfloat16).astype(jnp.float32)
            attended = attended + jnp.einsum('htu,uhd->thd', weights, split_heads(device_rows(value_f, qdevice - distance)))
        return (attended.reshape(TOK_DEV, D), row_peak, row_total)
    attended, peaks, totals = lax.map(forward_block, jnp.arange(N_TM, dtype=jnp.int32))
    attended = attended.reshape(TOKENS, D)
    squares = lax.optimization_barrier(jnp.sum(attended * attended, axis=1))
    inverse = lax.rsqrt(squares / D + NORM_EPS)
    prediction = attended * inverse[:, None] * gain
    position = jnp.arange(TOKENS, dtype=jnp.int32) % BLK
    chosen = jnp.any(jnp.repeat(mask_pos, BLK, axis=0) == position[:, None], axis=1)
    residual = jnp.where(chosen[:, None], prediction - teacher.astype(jnp.float32), 0.0)
    scaled = residual * gain
    cross_term = lax.optimization_barrier(jnp.sum(scaled * attended, axis=1))
    out_grad = (inverse[:, None] * scaled - attended * (inverse ** 3 * cross_term / D)[:, None]).astype(jnp.bfloat16)
    grad_f = out_grad.astype(jnp.float32)
    delta = lax.optimization_barrier(jnp.sum((grad_f * attended).reshape(TOKENS, HEADS, HD), axis=2))

    def pair_prob(qdevice, kdevice):
        scores, allowed = pair_scores(qdevice, kdevice)
        clipped = jnp.clip(qdevice, 0, N_TM - 1)
        expo = jnp.where(allowed[None], jnp.exp(scores - peaks[clipped][..., None]), 0.0)
        return expo / totals[clipped][..., None]

    def score_grad_of(qdevice, kdevice):
        prob = pair_prob(qdevice, kdevice)
        prob_grad = jnp.einsum('thd,uhd->htu', split_heads(device_rows(grad_f, qdevice)), split_heads(device_rows(value_f, kdevice)))
        score_grad = (prob * (prob_grad - device_rows(delta, qdevice).T[..., None])).astype(jnp.bfloat16).astype(jnp.float32)
        return (prob, score_grad)

    def query_block(qdevice):
        grad_block = jnp.zeros((TOK_DEV, HEADS, HD), jnp.float32)
        for distance in range(REACH + 1):
            kdevice = qdevice - distance
            prob, score_grad = score_grad_of(qdevice, kdevice)
            grad_block = grad_block + jnp.einsum('htu,uhd->thd', score_grad, split_heads(device_rows(key_f, kdevice))) * score_scale
        return grad_block.reshape(TOK_DEV, D)

    def key_block(kdevice):
        grad_keys = jnp.zeros((TOK_DEV, HEADS, HD), jnp.float32)
        grad_values = jnp.zeros((TOK_DEV, HEADS, HD), jnp.float32)
        for distance in range(REACH + 1):
            qdevice = kdevice + distance
            prob, score_grad = score_grad_of(qdevice, kdevice)
            grad_keys = grad_keys + jnp.einsum('htu,thd->uhd', score_grad, split_heads(device_rows(query_f, qdevice))) * score_scale
            weights = prob.astype(jnp.bfloat16).astype(jnp.float32)
            grad_values = grad_values + jnp.einsum('htu,thd->uhd', weights, split_heads(device_rows(grad_f, qdevice)))
        return (grad_keys.reshape(TOK_DEV, D), grad_values.reshape(TOK_DEV, D))
    query_grad = lax.map(query_block, jnp.arange(N_TM, dtype=jnp.int32)).reshape(TOKENS, D).astype(jnp.bfloat16)
    key_parts, value_parts = lax.map(key_block, jnp.arange(N_TM, dtype=jnp.int32))
    key_grad = key_parts.reshape(TOKENS, D).astype(jnp.bfloat16)
    value_acc = value_parts.reshape(TOKENS, D)
    padded_acc = jnp.concatenate([value_acc, jnp.zeros((KW - 1, D), jnp.float32)], 0)
    value_sum = jnp.zeros((TOKENS, D), jnp.float32)
    for tap_index in range(KW):
        value_sum = value_sum + conv_weight[tap_index] * padded_acc[tap_index:tap_index + TOKENS]
    value_grad = value_sum.astype(jnp.bfloat16)
    conv_grad = jnp.stack([lax.optimization_barrier(jnp.sum(value_acc * padded_in[KW - 1 - tap_index:KW - 1 - tap_index + TOKENS], axis=0)) for tap_index in range(KW)])
    return (query_grad, key_grad, value_grad, conv_grad)
```

```python
import functools

import jax
import jax.numpy as jnp
from jax import lax
from jax.experimental import pallas as pl
from jax.experimental.pallas import tpu as pltpu
from jax.sharding import PartitionSpec as P

HD = 128
BLK = 128
LOG2E = 1.4426950408889634
NEG_FILL = -1e30
NORM_EPS = 1e-06
MESH = pl.DeviceIdType.MESH
F32 = jnp.float32
BF16 = jnp.bfloat16


def dot_nt(a, b):
    return lax.dot_general(a, b, (((1,), (1,)), ((), ())), preferred_element_type=F32)


def dot_nn(a, b):
    return jnp.dot(a, b, preferred_element_type=F32)


def kernel(
    n,
    width,
    q_ref,
    k_ref,
    v_ref,
    t_ref,
    gain_ref,
    w_ref,
    bits_ref,
    pos_ref,
    dq_ref,
    dk_ref,
    dv_ref,
    dc_ref,
    kx,
    vx,
    qx,
    gx,
    stx,
    halo,
    extv,
    dvx,
    prob,
    att,
    mask,
    mask_t,
    stats,
    norm,
    norm_out,
    norm_in,
    tap_pair,
    tap_own,
    tap_all,
    send_sem,
    recv_sem,
    st_send,
    st_recv,
    misc_send,
    misc_recv,
    tap_send,
    tap_recv,
):
    rows, channels = q_ref.shape
    heads = channels // HD
    taps = w_ref.shape[0]
    win = bits_ref.shape[1]
    span = win * BLK
    total = kx.shape[1]
    me = lax.axis_index("tm")
    side = lax.axis_index("head")
    even = lax.rem(me, 2) == 0
    odd = lax.rem(me, 2) == 1
    chips = n // 2
    scale = HD ** (-0.5)
    scale2 = scale * LOG2E

    def cols(h):
        return pl.ds(pl.multiple_of(h * HD, HD), HD)

    def put(buf, lead, src, dst, count, send, recv, target):
        return pltpu.make_async_remote_copy(
            src_ref=buf.at[lead, pl.ds(src, count)],
            dst_ref=buf.at[lead, pl.ds(dst, count)],
            send_sem=send,
            recv_sem=recv,
            device_id={"tm": target},
            device_id_type=MESH,
        )

    own = total - rows

    def ahead_direct(buf, a, h):
        s, r = send_sem.at[a], recv_sem.at[a]
        return [
            (me + 2 < n, put(buf, h, own, BLK, rows, s.at[0, h], r.at[1, h], me + 2)),
            (even, put(buf, h, own, BLK + rows, rows, s.at[1, h], r.at[0, h], me + 1)),
            (
                odd & (me + 3 < n),
                put(buf, h, own + BLK, 0, BLK, s.at[1, h], r.at[2, h], me + 3),
            ),
        ]

    def ahead_relay(buf, a, h):
        s, r = send_sem.at[a], recv_sem.at[a]
        return [
            (odd & (me >= 2), put(buf, h, BLK, BLK + rows, rows, s.at[2, h], r.at[0, h], me - 1)),
            (even & (me >= 2), put(buf, h, BLK + BLK, 0, BLK, s.at[2, h], r.at[2, h], me + 1)),
        ]

    def back_direct(buf, a, h):
        s, r = send_sem.at[a], recv_sem.at[a]
        return [
            (me >= 2, put(buf, h, 0, 2 * rows, rows, s.at[0, h], r.at[1, h], me - 2)),
            (odd, put(buf, h, 0, rows, rows, s.at[1, h], r.at[0, h], me - 1)),
            (
                even & (me >= 3),
                put(buf, h, 0, 3 * rows, BLK, s.at[1, h], r.at[2, h], me - 3),
            ),
        ]

    def back_relay(buf, a, h):
        s, r = send_sem.at[a], recv_sem.at[a]
        return [
            (even & (me + 2 < n), put(buf, h, 2 * rows, rows, rows, s.at[2, h], r.at[0, h], me + 1)),
            (odd & (me + 2 < n), put(buf, h, 2 * rows, 3 * rows, BLK, s.at[2, h], r.at[2, h], me - 1)),
        ]

    def put_stat(src, dst, count, kind, slot, target):
        return pltpu.make_async_remote_copy(
            src_ref=stx.at[:, pl.ds(src, count)],
            dst_ref=stx.at[:, pl.ds(dst, count)],
            send_sem=st_send.at[kind],
            recv_sem=st_recv.at[slot],
            device_id={"tm": target},
            device_id_type=MESH,
        )

    def stat_direct():
        return [
            (me >= 2, put_stat(0, 2 * rows, rows, 0, 1, me - 2)),
            (odd, put_stat(0, rows, rows, 1, 0, me - 1)),
            (even & (me >= 3), put_stat(0, 3 * rows, BLK, 1, 2, me - 3)),
        ]

    def stat_relay():
        return [
            (even & (me + 2 < n), put_stat(2 * rows, rows, rows, 2, 0, me + 1)),
            (odd & (me + 2 < n), put_stat(2 * rows, 3 * rows, BLK, 2, 2, me - 1)),
        ]

    def start(copies):
        for ok, copy in copies:
            pl.when(ok)(copy.start)

    def sent(copies):
        for ok, copy in copies:
            pl.when(ok)(copy.wait_send)

    def got_ahead(buf, a, h, slot):
        dst, count = ((BLK + rows, rows), (BLK, rows), (0, BLK))[slot - 1]
        copy = put(buf, h, dst, dst, count, send_sem.at[a, 0, h], recv_sem.at[a, slot - 1, h], me)
        pl.when(me >= slot)(copy.wait_recv)

    def got_back(buf, a, h, slot):
        dst, count = slot * rows, BLK if slot == 3 else rows
        copy = put(buf, h, dst, dst, count, send_sem.at[a, 0, h], recv_sem.at[a, slot - 1, h], me)
        pl.when(me + slot < n)(copy.wait_recv)

    def got_stat(slot):
        dst, count = slot * rows, BLK if slot == 3 else rows
        pl.when(me + slot < n)(put_stat(dst, dst, count, 0, slot - 1, me).wait_recv)

    def each(body):
        def step(h, carry):
            body(h)
            return carry

        lax.fori_loop(0, heads, step, 0)

    barrier = pltpu.get_barrier_semaphore()

    def greet(i, carry):
        pl.semaphore_signal(
            barrier, inc=1, device_id={"tm": lax.rem(me + i, n)}, device_id_type=MESH
        )
        return carry

    lax.fori_loop(1, n, greet, 0)
    pl.semaphore_signal(barrier, inc=1, device_id={"head": 1 - side}, device_id_type=MESH)

    halo_rows = halo.shape[0]

    @functools.partial(each)
    def _(h):
        kx[h, own:total, :] = k_ref[:, cols(h)]

    pl.semaphore_wait(barrier, n)

    halo_copy = pltpu.make_async_remote_copy(
        src_ref=v_ref.at[pl.ds(rows - halo_rows, halo_rows)],
        dst_ref=halo,
        send_sem=misc_send.at[0],
        recv_sem=misc_recv.at[0],
        device_id={"tm": me + 1},
        device_id_type=MESH,
    )
    pl.when(me + 1 < n)(halo_copy.start)

    @functools.partial(each)
    def _(h):
        start(ahead_direct(kx, 0, h))

    for slot, (dst, count) in enumerate(((BLK + rows, rows), (BLK, rows), (0, BLK)), 1):

        @pl.when(me < slot)
        def _(dst=dst, count=count):
            @functools.partial(each)
            def _(h):
                kx[h, dst : dst + count, :] = jnp.zeros((count, HD), BF16)
                vx[h, dst : dst + count, :] = jnp.zeros((count, HD), BF16)

        back, back_count = slot * rows, BLK if slot == 3 else rows

        @pl.when(me + slot >= n)
        def _(dst=back, count=back_count):
            @functools.partial(each)
            def _(h):
                qx[h, dst : dst + count, :] = jnp.zeros((count, HD), BF16)
                gx[h, dst : dst + count, :] = jnp.zeros((count, HD), BF16)

            stx[:, dst : dst + count] = jnp.full((stx.shape[0], count), NEG_FILL, F32)

    @pl.when(me < 1)
    def _():
        halo[...] = jnp.zeros(halo.shape, BF16)

    pl.when(me >= 1)(halo_copy.wait_recv)

    @functools.partial(each)
    def _(h):
        extv[h, 0:8, :] = halo[:, cols(h)].astype(F32)[halo_rows - 8 :]
        extv[h, 8 : 8 + rows, :] = v_ref[:, cols(h)].astype(F32)
        acc = jnp.zeros((rows, HD), F32)
        for j in range(taps):
            acc = acc + w_ref[j : j + 1, cols(h)] * extv[h, 8 - j : 8 - j + rows, :]
        vx[h, own:total, :] = acc.astype(BF16)
        start(ahead_direct(vx, 1, h))

    @functools.partial(each)
    def _(h):
        qx[h, 0:rows, :] = q_ref[:, cols(h)]
        start(back_direct(qx, 2, h))

    line = lax.broadcasted_iota(jnp.int32, (BLK, BLK), 0)
    lane = lax.broadcasted_iota(jnp.int32, (BLK, BLK), 1)
    for i in range(rows // BLK):
        for r in range(win):
            bit = bits_ref[i, r] > 0
            there = me * (rows // BLK) + i - r >= 0
            part = jnp.full((BLK, BLK), jnp.where(bit & there, 0.0, NEG_FILL), F32)
            if r == 0:
                part = jnp.where(lane <= line, part, NEG_FILL)
            mask[i, :, (win - 1 - r) * BLK : (win - r) * BLK] = part
            stx[3 * heads + r : 3 * heads + r + 1, i * BLK : (i + 1) * BLK] = jnp.full(
                (1, BLK), jnp.where(bit, 0.0, NEG_FILL), F32
            )

    stats[...] = jnp.zeros(stats.shape, F32)
    norm[...] = jnp.zeros(norm.shape, F32)

    def relay_kv(h):
        got_ahead(kx, 0, h, 2)
        start(ahead_relay(kx, 0, h))
        got_ahead(vx, 1, h, 2)
        start(ahead_relay(vx, 1, h))

    relay_kv(0)

    @functools.partial(each)
    def _(h):
        pl.when(h + 1 < heads)(lambda: relay_kv(h + 1))
        got_ahead(kx, 0, h, 1)
        got_ahead(kx, 0, h, 3)
        got_ahead(vx, 1, h, 1)
        got_ahead(vx, 1, h, 3)
        gain = gain_ref[:, cols(h)]
        for i in range(rows // BLK):
            here = slice(i * BLK, (i + 1) * BLK)
            window = slice(i * BLK, i * BLK + span)
            s = dot_nt(qx[h, here, :], kx[h, window, :]) * scale2 + mask[i]
            peak = jnp.max(s, axis=1, keepdims=True)
            e = jnp.exp2(s - peak)
            inv = 1.0 / jnp.sum(e, axis=1, keepdims=True)
            p = e * inv
            prob[h, i] = p
            o = dot_nn(p.astype(BF16), vx[h, window, :])
            att[h, here, :] = o
            stats[here, :] = jnp.where(
                lane == h, -peak, jnp.where(lane == heads + h, inv, stats[here, :])
            )
            og = o * gain
            norm[0, here, :] += o * o
            norm[1, here, :] += og * og
            norm[2, here, :] += og * t_ref[here, cols(h)].astype(F32)

    big_lane = lax.broadcasted_iota(jnp.int32, (rows, HD), 1)
    sums = [jnp.sum(norm[i], axis=1, keepdims=True) for i in range(3)]
    norm_out[...] = jnp.where(
        big_lane == 0, sums[0], jnp.where(big_lane == 1, sums[1], sums[2])
    )
    norm_copy = pltpu.make_async_remote_copy(
        src_ref=norm_out,
        dst_ref=norm_in,
        send_sem=misc_send.at[1],
        recv_sem=misc_recv.at[1],
        device_id={"head": 1 - side},
        device_id_type=MESH,
    )
    norm_copy.start()
    chosen = jnp.concatenate(
        [
            jnp.max(
                jnp.where(
                    pos_ref[i : i + 1, :]
                    == lax.broadcasted_iota(jnp.int32, (BLK, pos_ref.shape[1]), 0),
                    1.0,
                    0.0,
                ),
                axis=1,
                keepdims=True,
            )
            for i in range(rows // BLK)
        ],
        axis=0,
    )
    norm_copy.wait_recv()
    both = norm_out[...] + norm_in[...]
    inverse = lax.rsqrt(both[:, 0:1] / width + NORM_EPS)
    cross = chosen * (inverse * both[:, 1:2] - both[:, 2:3])
    factor = inverse * inverse * inverse * cross / width

    @functools.partial(each)
    def _(h):
        gain = gain_ref[:, cols(h)]
        o = att[h]
        scaled = (o * inverse * gain - t_ref[:, cols(h)].astype(F32)) * chosen * gain
        grad = (inverse * scaled - o * factor).astype(BF16)
        gx[h, 0:rows, :] = grad
        start(back_direct(gx, 3, h))
        delta = jnp.sum(grad.astype(F32) * o, axis=1, keepdims=True)
        stats[...] = jnp.where(big_lane == 2 * heads + h, delta, stats[...])

    stx[0 : 3 * heads, 0:rows] = stats[...].T[0 : 3 * heads]
    stx[3 * heads + win :, 0:rows] = jnp.zeros((stx.shape[0] - 3 * heads - win, rows), F32)
    start(stat_direct())

    @functools.partial(each)
    def _(h):
        got_back(qx, 2, h, 2)
        start(back_relay(qx, 2, h))
        got_back(gx, 3, h, 2)
        start(back_relay(gx, 3, h))
        for i in range(rows // BLK):
            here = slice(i * BLK, (i + 1) * BLK)
            window = slice(i * BLK, i * BLK + span)
            grad = gx[h, here, :]
            delta = jnp.sum(grad.astype(F32) * att[h, here, :], axis=1, keepdims=True)
            dp = dot_nt(grad, vx[h, window, :])
            ds = (prob[h, i] * (dp - delta)).astype(BF16)
            dq_ref[here, cols(h)] = (dot_nn(ds, kx[h, window, :]) * scale).astype(BF16)

    got_stat(2)
    start(stat_relay())
    got_stat(1)
    got_stat(3)
    for i in range(rows // BLK):
        for r in range(win):
            part = jnp.broadcast_to(
                stx[3 * heads + r : 3 * heads + r + 1, (i + r) * BLK : (i + r + 1) * BLK],
                (BLK, BLK),
            )
            if r == 0:
                part = jnp.where(line <= lane, part, NEG_FILL)
            mask_t[i, :, r * BLK : (r + 1) * BLK] = part

    @functools.partial(each)
    def _(h):
        got_back(qx, 2, h, 1)
        got_back(qx, 2, h, 3)
        got_back(gx, 3, h, 1)
        got_back(gx, 3, h, 3)
        for i in range(rows // BLK):
            here = slice(own + i * BLK, own + (i + 1) * BLK)
            out = slice(i * BLK, (i + 1) * BLK)
            window = slice(i * BLK, i * BLK + span)
            peak = stx[pl.ds(h, 1), window]
            inv = stx[pl.ds(heads + h, 1), window]
            delta = stx[pl.ds(2 * heads + h, 1), window]
            s = dot_nt(kx[h, here, :], qx[h, window, :]) * scale2 + mask_t[i]
            p = jnp.exp2(s + peak) * inv
            dvx[h, out, :] = dot_nn(p.astype(BF16), gx[h, window, :])
            dp = dot_nt(vx[h, here, :], gx[h, window, :])
            ds = (p * (dp - delta)).astype(BF16)
            dk_ref[out, cols(h)] = (dot_nn(ds, qx[h, window, :]) * scale).astype(BF16)
        for j in range(taps):
            tap_own[j : j + 1, cols(h)] = jnp.sum(
                dvx[h, 0:rows, :] * extv[h, 8 - j : 8 - j + rows, :], axis=0, keepdims=True
            )

    rim_copy = pltpu.make_async_remote_copy(
        src_ref=dvx.at[:, pl.ds(0, 8)],
        dst_ref=dvx.at[:, pl.ds(rows, 8)],
        send_sem=misc_send.at[2],
        recv_sem=misc_recv.at[2],
        device_id={"tm": me - 1},
        device_id_type=MESH,
    )
    pair_copy = pltpu.make_async_remote_copy(
        src_ref=tap_own,
        dst_ref=tap_pair,
        send_sem=misc_send.at[3],
        recv_sem=misc_recv.at[3],
        device_id={"tm": me + 1 - 2 * lax.rem(me, 2)},
        device_id_type=MESH,
    )
    pair_copy.start()
    pl.when(me >= 1)(rim_copy.start)
    core = lax.rem(me, 2)
    chip = me // 2
    pair_copy.wait_recv()
    tap_all[chip] = tap_own[...] + tap_pair[...]

    def share(k):
        return pltpu.make_async_remote_copy(
            src_ref=tap_all.at[chip],
            dst_ref=tap_all.at[chip],
            send_sem=tap_send.at[k],
            recv_sem=tap_recv.at[k],
            device_id={"tm": lax.rem(chip + k, chips) * 2 + core},
            device_id_type=MESH,
        )

    def got_share(k):
        source = lax.rem(chip + chips - k, chips)
        return pltpu.make_async_remote_copy(
            src_ref=tap_all.at[source],
            dst_ref=tap_all.at[source],
            send_sem=tap_send.at[k],
            recv_sem=tap_recv.at[k],
            device_id={"tm": me},
            device_id_type=MESH,
        )

    def run(first, last, body):
        def step(k, carry):
            body(k)
            return carry

        lax.fori_loop(first, last, step, 0)

    run(1, chips, lambda k: share(k).start())

    @pl.when(me + 1 >= n)
    def _():
        dvx[:, rows : rows + 8, :] = jnp.zeros((heads, 8, HD), F32)

    pl.when(me + 1 < n)(rim_copy.wait_recv)

    @functools.partial(each)
    def _(h):
        acc = jnp.zeros((rows, HD), F32)
        for j in range(taps):
            acc = acc + w_ref[j : j + 1, cols(h)] * dvx[h, j : j + rows, :]
        dv_ref[:, cols(h)] = acc.astype(BF16)

    @functools.partial(each)
    def _(h):
        sent(ahead_direct(kx, 0, h))
        sent(ahead_relay(kx, 0, h))
        sent(ahead_direct(vx, 1, h))
        sent(ahead_relay(vx, 1, h))
        sent(back_direct(qx, 2, h))
        sent(back_relay(qx, 2, h))
        sent(back_direct(gx, 3, h))
        sent(back_relay(gx, 3, h))

    sent(stat_direct())
    sent(stat_relay())
    pl.when(me + 1 < n)(halo_copy.wait_send)
    norm_copy.wait_send()
    pl.when(me >= 1)(rim_copy.wait_send)
    pair_copy.wait_send()
    run(1, chips, lambda k: got_share(k).wait_recv())
    acc = tap_all[0]
    for c in range(1, chips):
        acc = acc + tap_all[c]
    dc_ref[...] = acc
    run(1, chips, lambda k: share(k).wait_send())


def body(n, parts, queries, keys, values_in, teacher, gain, conv_weight, block_bits, mask_pos):
    rows, channels = queries.shape
    heads = channels // HD
    taps = conv_weight.shape[0]
    win = block_bits.shape[1]
    span = win * BLK
    total = span + rows - BLK
    blocks = rows // BLK
    stat_rows = -(-(3 * heads + win) // 8) * 8
    vmem = pl.BlockSpec(memory_space=pltpu.VMEM)
    smem = pl.BlockSpec(memory_space=pltpu.SMEM)
    dma = pltpu.SemaphoreType.DMA
    return pl.pallas_call(
        functools.partial(kernel, n, channels * parts),
        out_shape=(
            jax.ShapeDtypeStruct((rows, channels), BF16),
            jax.ShapeDtypeStruct((rows, channels), BF16),
            jax.ShapeDtypeStruct((rows, channels), BF16),
            jax.ShapeDtypeStruct((taps, channels), F32),
        ),
        in_specs=[vmem] * 6 + [smem, vmem],
        out_specs=(vmem,) * 4,
        scratch_shapes=[
            pltpu.VMEM((heads, total, HD), BF16),
            pltpu.VMEM((heads, total, HD), BF16),
            pltpu.VMEM((heads, total, HD), BF16),
            pltpu.VMEM((heads, total, HD), BF16),
            pltpu.VMEM((stat_rows, total), F32),
            pltpu.VMEM((16, channels), BF16),
            pltpu.VMEM((heads, rows + 8, HD), F32),
            pltpu.VMEM((heads, rows + 8, HD), F32),
            pltpu.VMEM((heads, blocks, BLK, span), F32),
            pltpu.VMEM((heads, rows, HD), F32),
            pltpu.VMEM((blocks, BLK, span), F32),
            pltpu.VMEM((blocks, BLK, span), F32),
            pltpu.VMEM((rows, HD), F32),
            pltpu.VMEM((3, rows, HD), F32),
            pltpu.VMEM((rows, HD), F32),
            pltpu.VMEM((rows, HD), F32),
            pltpu.VMEM((taps, channels), F32),
            pltpu.VMEM((taps, channels), F32),
            pltpu.VMEM((n // 2, taps, channels), F32),
            dma((4, 3, heads)),
            dma((4, 3, heads)),
            dma((3,)),
            dma((3,)),
            dma((4,)),
            dma((4,)),
            dma((n // 2,)),
            dma((n // 2,)),
        ],
        compiler_params=pltpu.CompilerParams(
            collective_id=0, has_side_effects=True, vmem_limit_bytes=48 * 1024 * 1024
        ),
    )(queries, keys, values_in, teacher, gain.reshape(1, channels), conv_weight, block_bits, mask_pos)


def solution(mesh):
    placed = (
        P("tm", "head"),
        P("tm", "head"),
        P("tm", "head"),
        P("tm", "head"),
        P("head"),
        P(None, "head"),
        P("tm", None),
        P("tm", None),
    )
    return jax.shard_map(
        functools.partial(body, mesh.shape["tm"], mesh.shape["head"]),
        mesh=mesh,
        in_specs=placed,
        out_specs=(P("tm", "head"), P("tm", "head"), P("tm", "head"), P(None, "head")),
        check_vma=False,
    )
```

```python
import functools

import jax
import jax.numpy as jnp
from jax import lax
from jax.experimental import pallas as pl
from jax.experimental.pallas import tpu as pltpu
from jax.sharding import PartitionSpec as P

HD = 128
BLK = 128
LOG2E = 1.4426950408889634
NEG_FILL = -1e30
NORM_EPS = 1e-06
MESH = pl.DeviceIdType.MESH
F32 = jnp.float32
BF16 = jnp.bfloat16


def dot_nt(a, b):
    return lax.dot_general(a, b, (((1,), (1,)), ((), ())), preferred_element_type=F32)


def dot_nn(a, b):
    return jnp.dot(a, b, preferred_element_type=F32)


def kernel(
    n,
    width,
    q_hbm,
    k_hbm,
    v_hbm,
    t_hbm,
    gain_hbm,
    w_hbm,
    bits_ref,
    pos_hbm,
    dq_ref,
    dk_ref,
    dv_ref,
    dc_ref,
    v_ref,
    t_ref,
    gain_ref,
    w_ref,
    pos_ref,
    kx,
    vx,
    qx,
    gx,
    stx,
    halo,
    extv,
    dvx,
    prob,
    att,
    mask,
    mask_t,
    stats,
    norm,
    norm_out,
    norm_in,
    tap_pair,
    tap_own,
    tap_all,
    send_sem,
    recv_sem,
    st_send,
    st_recv,
    misc_send,
    misc_recv,
    tap_send,
    tap_recv,
    head_sem,
    in_sem,
):
    rows, channels = q_hbm.shape
    heads = channels // HD
    taps = w_ref.shape[0]
    win = bits_ref.shape[1]
    span = win * BLK
    total = kx.shape[1]
    me = lax.axis_index("tm")
    side = lax.axis_index("head")
    even = lax.rem(me, 2) == 0
    odd = lax.rem(me, 2) == 1
    chips = n // 2
    scale = HD ** (-0.5)
    scale2 = scale * LOG2E

    def cols(h):
        return pl.ds(pl.multiple_of(h * HD, HD), HD)

    def put(buf, lead, src, dst, count, send, recv, target):
        return pltpu.make_async_remote_copy(
            src_ref=buf.at[lead, pl.ds(src, count)],
            dst_ref=buf.at[lead, pl.ds(dst, count)],
            send_sem=send,
            recv_sem=recv,
            device_id={"tm": target},
            device_id_type=MESH,
        )

    own = total - rows

    def ahead_direct(buf, a, h):
        s, r = send_sem.at[a], recv_sem.at[a]
        return [
            (me + 2 < n, put(buf, h, own, BLK, rows, s.at[0, h], r.at[1, h], me + 2)),
            (even, put(buf, h, own, BLK + rows, rows, s.at[1, h], r.at[0, h], me + 1)),
            (
                odd & (me + 3 < n),
                put(buf, h, own + BLK, 0, BLK, s.at[1, h], r.at[2, h], me + 3),
            ),
        ]

    def ahead_relay(buf, a, h):
        s, r = send_sem.at[a], recv_sem.at[a]
        return [
            (odd & (me >= 2), put(buf, h, BLK, BLK + rows, rows, s.at[2, h], r.at[0, h], me - 1)),
            (even & (me >= 2), put(buf, h, BLK + BLK, 0, BLK, s.at[2, h], r.at[2, h], me + 1)),
        ]

    def back_direct(buf, a, h):
        s, r = send_sem.at[a], recv_sem.at[a]
        return [
            (me >= 2, put(buf, h, 0, 2 * rows, rows, s.at[0, h], r.at[1, h], me - 2)),
            (odd, put(buf, h, 0, rows, rows, s.at[1, h], r.at[0, h], me - 1)),
            (
                even & (me >= 3),
                put(buf, h, 0, 3 * rows, BLK, s.at[1, h], r.at[2, h], me - 3),
            ),
        ]

    def back_relay(buf, a, h):
        s, r = send_sem.at[a], recv_sem.at[a]
        return [
            (even & (me + 2 < n), put(buf, h, 2 * rows, rows, rows, s.at[2, h], r.at[0, h], me + 1)),
            (odd & (me + 2 < n), put(buf, h, 2 * rows, 3 * rows, BLK, s.at[2, h], r.at[2, h], me - 1)),
        ]

    def put_stat(src, dst, count, kind, slot, target):
        return pltpu.make_async_remote_copy(
            src_ref=stx.at[:, pl.ds(src, count)],
            dst_ref=stx.at[:, pl.ds(dst, count)],
            send_sem=st_send.at[kind],
            recv_sem=st_recv.at[slot],
            device_id={"tm": target},
            device_id_type=MESH,
        )

    def stat_direct():
        return [
            (me >= 2, put_stat(0, 2 * rows, rows, 0, 1, me - 2)),
            (odd, put_stat(0, rows, rows, 1, 0, me - 1)),
            (even & (me >= 3), put_stat(0, 3 * rows, BLK, 1, 2, me - 3)),
        ]

    def stat_relay():
        return [
            (even & (me + 2 < n), put_stat(2 * rows, rows, rows, 2, 0, me + 1)),
            (odd & (me + 2 < n), put_stat(2 * rows, 3 * rows, BLK, 2, 2, me - 1)),
        ]

    def start(copies):
        for ok, copy in copies:
            pl.when(ok)(copy.start)

    def sent(copies):
        for ok, copy in copies:
            pl.when(ok)(copy.wait_send)

    def got_ahead(buf, a, h, slot):
        dst, count = ((BLK + rows, rows), (BLK, rows), (0, BLK))[slot - 1]
        copy = put(buf, h, dst, dst, count, send_sem.at[a, 0, h], recv_sem.at[a, slot - 1, h], me)
        pl.when(me >= slot)(copy.wait_recv)

    def got_back(buf, a, h, slot):
        dst, count = slot * rows, BLK if slot == 3 else rows
        copy = put(buf, h, dst, dst, count, send_sem.at[a, 0, h], recv_sem.at[a, slot - 1, h], me)
        pl.when(me + slot < n)(copy.wait_recv)

    def got_stat(slot):
        dst, count = slot * rows, BLK if slot == 3 else rows
        pl.when(me + slot < n)(put_stat(dst, dst, count, 0, slot - 1, me).wait_recv)

    def each(body):
        def step(h, carry):
            body(h)
            return carry

        lax.fori_loop(0, heads, step, 0)

    barrier = pltpu.get_barrier_semaphore()

    def greet(i, carry):
        pl.semaphore_signal(
            barrier, inc=1, device_id={"tm": lax.rem(me + i, n)}, device_id_type=MESH
        )
        return carry

    lax.fori_loop(1, n, greet, 0)
    pl.semaphore_signal(barrier, inc=1, device_id={"head": 1 - side}, device_id_type=MESH)

    halo_rows = halo.shape[0]

    def load_key(h):
        return pltpu.make_async_copy(
            k_hbm.at[:, cols(h)], kx.at[h, pl.ds(own, rows)], head_sem.at[0, h]
        )

    def load_query(h):
        return pltpu.make_async_copy(
            q_hbm.at[:, cols(h)], qx.at[h, pl.ds(0, rows)], head_sem.at[1, h]
        )

    loads = [
        pltpu.make_async_copy(a, b, in_sem.at[i])
        for i, (a, b) in enumerate(
            (
                (v_hbm, v_ref),
                (w_hbm, w_ref),
                (gain_hbm, gain_ref),
                (pos_hbm, pos_ref),
                (t_hbm, t_ref),
            )
        )
    ]
    loads[0].start()
    each(lambda h: load_key(h).start())
    for load in loads[1:]:
        load.start()
    each(lambda h: load_query(h).start())
    loads[0].wait()
    pl.semaphore_wait(barrier, n)

    halo_copy = pltpu.make_async_remote_copy(
        src_ref=v_ref.at[pl.ds(rows - halo_rows, halo_rows)],
        dst_ref=halo,
        send_sem=misc_send.at[0],
        recv_sem=misc_recv.at[0],
        device_id={"tm": me + 1},
        device_id_type=MESH,
    )
    pl.when(me + 1 < n)(halo_copy.start)

    first = heads // 2

    @functools.partial(each)
    def _(h):
        load_key(h).wait()
        pl.when(h < first)(lambda: start(ahead_direct(kx, 0, h)))

    for load in loads[1:]:
        load.wait()

    for slot, (dst, count) in enumerate(((BLK + rows, rows), (BLK, rows), (0, BLK)), 1):

        @pl.when(me < slot)
        def _(dst=dst, count=count):
            @functools.partial(each)
            def _(h):
                kx[h, dst : dst + count, :] = jnp.zeros((count, HD), BF16)
                vx[h, dst : dst + count, :] = jnp.zeros((count, HD), BF16)

        back, back_count = slot * rows, BLK if slot == 3 else rows

        @pl.when(me + slot >= n)
        def _(dst=back, count=back_count):
            @functools.partial(each)
            def _(h):
                qx[h, dst : dst + count, :] = jnp.zeros((count, HD), BF16)
                gx[h, dst : dst + count, :] = jnp.zeros((count, HD), BF16)

            stx[:, dst : dst + count] = jnp.full((stx.shape[0], count), NEG_FILL, F32)

    @pl.when(me < 1)
    def _():
        halo[...] = jnp.zeros(halo.shape, BF16)

    pl.when(me >= 1)(halo_copy.wait_recv)

    @functools.partial(each)
    def _(h):
        extv[h, 0:8, :] = halo[:, cols(h)].astype(F32)[halo_rows - 8 :]
        extv[h, 8 : 8 + rows, :] = v_ref[:, cols(h)].astype(F32)
        acc = jnp.zeros((rows, HD), F32)
        for j in range(taps):
            acc = acc + w_ref[j : j + 1, cols(h)] * extv[h, 8 - j : 8 - j + rows, :]
        vx[h, own:total, :] = acc.astype(BF16)
        start(ahead_direct(vx, 1, h))
        pl.when(h + first < heads)(lambda: start(ahead_direct(kx, 0, h + first)))

    each(lambda h: load_query(h).wait())

    line = lax.broadcasted_iota(jnp.int32, (BLK, BLK), 0)
    lane = lax.broadcasted_iota(jnp.int32, (BLK, BLK), 1)
    for i in range(rows // BLK):
        for r in range(win):
            bit = bits_ref[i, r] > 0
            there = me * (rows // BLK) + i - r >= 0
            part = jnp.full((BLK, BLK), jnp.where(bit & there, 0.0, NEG_FILL), F32)
            if r == 0:
                part = jnp.where(lane <= line, part, NEG_FILL)
            mask[i, :, (win - 1 - r) * BLK : (win - r) * BLK] = part
            stx[3 * heads + r : 3 * heads + r + 1, i * BLK : (i + 1) * BLK] = jnp.full(
                (1, BLK), jnp.where(bit, 0.0, NEG_FILL), F32
            )

    stats[...] = jnp.zeros(stats.shape, F32)
    norm[...] = jnp.zeros(norm.shape, F32)

    def relay_kv(h):
        got_ahead(kx, 0, h, 2)
        start(ahead_relay(kx, 0, h))
        got_ahead(vx, 1, h, 2)
        start(ahead_relay(vx, 1, h))

    relay_kv(0)

    @functools.partial(each)
    def _(h):
        pl.when(h + 1 < heads)(lambda: relay_kv(h + 1))
        got_ahead(kx, 0, h, 1)
        got_ahead(kx, 0, h, 3)
        got_ahead(vx, 1, h, 1)
        got_ahead(vx, 1, h, 3)

        @pl.when(h >= first)
        def _():
            start(back_direct(qx, 2, 2 * (h - first)))
            start(back_direct(qx, 2, 2 * (h - first) + 1))

        gain = gain_ref[:, cols(h)]
        for i in range(rows // BLK):
            here = slice(i * BLK, (i + 1) * BLK)
            window = slice(i * BLK, i * BLK + span)
            s = dot_nt(qx[h, here, :], kx[h, window, :]) * scale2 + mask[i]
            peak = jnp.max(s, axis=1, keepdims=True)
            e = jnp.exp2(s - peak)
            inv = 1.0 / jnp.sum(e, axis=1, keepdims=True)
            p = e * inv
            prob[h, i] = p
            o = dot_nn(p.astype(BF16), vx[h, window, :])
            att[h, here, :] = o
            stats[here, :] = jnp.where(
                lane == h, -peak, jnp.where(lane == heads + h, inv, stats[here, :])
            )
            og = o * gain
            norm[0, here, :] += o * o
            norm[1, here, :] += og * og
            norm[2, here, :] += og * t_ref[here, cols(h)].astype(F32)

    big_lane = lax.broadcasted_iota(jnp.int32, (rows, HD), 1)
    sums = [jnp.sum(norm[i], axis=1, keepdims=True) for i in range(3)]
    norm_out[...] = jnp.where(
        big_lane == 0, sums[0], jnp.where(big_lane == 1, sums[1], sums[2])
    )
    norm_copy = pltpu.make_async_remote_copy(
        src_ref=norm_out,
        dst_ref=norm_in,
        send_sem=misc_send.at[1],
        recv_sem=misc_recv.at[1],
        device_id={"head": 1 - side},
        device_id_type=MESH,
    )
    norm_copy.start()
    chosen = jnp.concatenate(
        [
            jnp.max(
                jnp.where(
                    pos_ref[i : i + 1, :]
                    == lax.broadcasted_iota(jnp.int32, (BLK, pos_ref.shape[1]), 0),
                    1.0,
                    0.0,
                ),
                axis=1,
                keepdims=True,
            )
            for i in range(rows // BLK)
        ],
        axis=0,
    )
    norm_copy.wait_recv()
    both = norm_out[...] + norm_in[...]
    inverse = lax.rsqrt(both[:, 0:1] / width + NORM_EPS)
    cross = chosen * (inverse * both[:, 1:2] - both[:, 2:3])
    factor = inverse * inverse * inverse * cross / width

    @functools.partial(each)
    def _(h):
        gain = gain_ref[:, cols(h)]
        o = att[h]
        scaled = (o * inverse * gain - t_ref[:, cols(h)].astype(F32)) * chosen * gain
        grad = (inverse * scaled - o * factor).astype(BF16)
        gx[h, 0:rows, :] = grad
        delta = jnp.sum(grad.astype(F32) * o, axis=1, keepdims=True)
        stats[...] = jnp.where(big_lane == 2 * heads + h, delta, stats[...])

    stx[0 : 3 * heads, 0:rows] = stats[...].T[0 : 3 * heads]
    stx[3 * heads + win :, 0:rows] = jnp.zeros((stx.shape[0] - 3 * heads - win, rows), F32)
    start(stat_direct())
    each(lambda h: start(back_direct(gx, 3, h)))

    @functools.partial(each)
    def _(h):
        for i in range(rows // BLK):
            here = slice(i * BLK, (i + 1) * BLK)
            window = slice(i * BLK, i * BLK + span)
            grad = gx[h, here, :]
            delta = jnp.sum(grad.astype(F32) * att[h, here, :], axis=1, keepdims=True)
            dp = dot_nt(grad, vx[h, window, :])
            ds = (prob[h, i] * (dp - delta)).astype(BF16)
            dq_ref[here, cols(h)] = (dot_nn(ds, kx[h, window, :]) * scale).astype(BF16)

    def relay_qg(h):
        got_back(qx, 2, h, 2)
        start(back_relay(qx, 2, h))
        got_back(gx, 3, h, 2)
        start(back_relay(gx, 3, h))

    got_stat(2)
    start(stat_relay())
    relay_qg(0)
    got_stat(1)
    got_stat(3)
    for i in range(rows // BLK):
        for r in range(win):
            part = jnp.broadcast_to(
                stx[3 * heads + r : 3 * heads + r + 1, (i + r) * BLK : (i + r + 1) * BLK],
                (BLK, BLK),
            )
            if r == 0:
                part = jnp.where(line <= lane, part, NEG_FILL)
            mask_t[i, :, r * BLK : (r + 1) * BLK] = part

    @functools.partial(each)
    def _(h):
        pl.when(h + 1 < heads)(lambda: relay_qg(h + 1))
        got_back(qx, 2, h, 1)
        got_back(qx, 2, h, 3)
        got_back(gx, 3, h, 1)
        got_back(gx, 3, h, 3)
        for i in range(rows // BLK):
            here = slice(own + i * BLK, own + (i + 1) * BLK)
            out = slice(i * BLK, (i + 1) * BLK)
            window = slice(i * BLK, i * BLK + span)
            peak = stx[pl.ds(h, 1), window]
            inv = stx[pl.ds(heads + h, 1), window]
            delta = stx[pl.ds(2 * heads + h, 1), window]
            s = dot_nt(kx[h, here, :], qx[h, window, :]) * scale2 + mask_t[i]
            p = jnp.exp2(s + peak) * inv
            dvx[h, out, :] = dot_nn(p.astype(BF16), gx[h, window, :])
            dp = dot_nt(vx[h, here, :], gx[h, window, :])
            ds = (p * (dp - delta)).astype(BF16)
            dk_ref[out, cols(h)] = (dot_nn(ds, qx[h, window, :]) * scale).astype(BF16)
        for j in range(taps):
            tap_own[j : j + 1, cols(h)] = jnp.sum(
                dvx[h, 0:rows, :] * extv[h, 8 - j : 8 - j + rows, :], axis=0, keepdims=True
            )

    rim_copy = pltpu.make_async_remote_copy(
        src_ref=dvx.at[:, pl.ds(0, 8)],
        dst_ref=dvx.at[:, pl.ds(rows, 8)],
        send_sem=misc_send.at[2],
        recv_sem=misc_recv.at[2],
        device_id={"tm": me - 1},
        device_id_type=MESH,
    )
    pair_copy = pltpu.make_async_remote_copy(
        src_ref=tap_own,
        dst_ref=tap_pair,
        send_sem=misc_send.at[3],
        recv_sem=misc_recv.at[3],
        device_id={"tm": me + 1 - 2 * lax.rem(me, 2)},
        device_id_type=MESH,
    )
    pair_copy.start()
    pl.when(me >= 1)(rim_copy.start)
    core = lax.rem(me, 2)
    chip = me // 2
    pair_copy.wait_recv()
    tap_all[chip] = tap_own[...] + tap_pair[...]

    def share(k):
        return pltpu.make_async_remote_copy(
            src_ref=tap_all.at[chip],
            dst_ref=tap_all.at[chip],
            send_sem=tap_send.at[k],
            recv_sem=tap_recv.at[k],
            device_id={"tm": lax.rem(chip + k, chips) * 2 + core},
            device_id_type=MESH,
        )

    def got_share(k):
        source = lax.rem(chip + chips - k, chips)
        return pltpu.make_async_remote_copy(
            src_ref=tap_all.at[source],
            dst_ref=tap_all.at[source],
            send_sem=tap_send.at[k],
            recv_sem=tap_recv.at[k],
            device_id={"tm": me},
            device_id_type=MESH,
        )

    def run(first, last, body):
        def step(k, carry):
            body(k)
            return carry

        lax.fori_loop(first, last, step, 0)

    run(1, chips, lambda k: share(k).start())

    @pl.when(me + 1 >= n)
    def _():
        dvx[:, rows : rows + 8, :] = jnp.zeros((heads, 8, HD), F32)

    pl.when(me + 1 < n)(rim_copy.wait_recv)

    @functools.partial(each)
    def _(h):
        acc = jnp.zeros((rows, HD), F32)
        for j in range(taps):
            acc = acc + w_ref[j : j + 1, cols(h)] * dvx[h, j : j + rows, :]
        dv_ref[:, cols(h)] = acc.astype(BF16)

    @functools.partial(each)
    def _(h):
        sent(ahead_direct(kx, 0, h))
        sent(ahead_relay(kx, 0, h))
        sent(ahead_direct(vx, 1, h))
        sent(ahead_relay(vx, 1, h))
        sent(back_direct(qx, 2, h))
        sent(back_relay(qx, 2, h))
        sent(back_direct(gx, 3, h))
        sent(back_relay(gx, 3, h))

    sent(stat_direct())
    sent(stat_relay())
    pl.when(me + 1 < n)(halo_copy.wait_send)
    norm_copy.wait_send()
    pl.when(me >= 1)(rim_copy.wait_send)
    pair_copy.wait_send()
    run(1, chips, lambda k: got_share(k).wait_recv())
    acc = tap_all[0]
    for c in range(1, chips):
        acc = acc + tap_all[c]
    dc_ref[...] = acc
    run(1, chips, lambda k: share(k).wait_send())


def body(n, parts, queries, keys, values_in, teacher, gain, conv_weight, block_bits, mask_pos):
    rows, channels = queries.shape
    heads = channels // HD
    taps = conv_weight.shape[0]
    win = block_bits.shape[1]
    span = win * BLK
    total = span + rows - BLK
    blocks = rows // BLK
    stat_rows = -(-(3 * heads + win) // 8) * 8
    vmem = pl.BlockSpec(memory_space=pltpu.VMEM)
    hbm = pl.BlockSpec(memory_space=pl.ANY)
    smem = pl.BlockSpec(memory_space=pltpu.SMEM)
    dma = pltpu.SemaphoreType.DMA
    return pl.pallas_call(
        functools.partial(kernel, n, channels * parts),
        out_shape=(
            jax.ShapeDtypeStruct((rows, channels), BF16),
            jax.ShapeDtypeStruct((rows, channels), BF16),
            jax.ShapeDtypeStruct((rows, channels), BF16),
            jax.ShapeDtypeStruct((taps, channels), F32),
        ),
        in_specs=[hbm] * 6 + [smem, hbm],
        out_specs=(vmem,) * 4,
        scratch_shapes=[
            pltpu.VMEM((rows, channels), BF16),
            pltpu.VMEM((rows, channels), BF16),
            pltpu.VMEM((1, channels), F32),
            pltpu.VMEM((taps, channels), F32),
            pltpu.VMEM(mask_pos.shape, jnp.int32),
            pltpu.VMEM((heads, total, HD), BF16),
            pltpu.VMEM((heads, total, HD), BF16),
            pltpu.VMEM((heads, total, HD), BF16),
            pltpu.VMEM((heads, total, HD), BF16),
            pltpu.VMEM((stat_rows, total), F32),
            pltpu.VMEM((16, channels), BF16),
            pltpu.VMEM((heads, rows + 8, HD), F32),
            pltpu.VMEM((heads, rows + 8, HD), F32),
            pltpu.VMEM((heads, blocks, BLK, span), F32),
            pltpu.VMEM((heads, rows, HD), F32),
            pltpu.VMEM((blocks, BLK, span), F32),
            pltpu.VMEM((blocks, BLK, span), F32),
            pltpu.VMEM((rows, HD), F32),
            pltpu.VMEM((3, rows, HD), F32),
            pltpu.VMEM((rows, HD), F32),
            pltpu.VMEM((rows, HD), F32),
            pltpu.VMEM((taps, channels), F32),
            pltpu.VMEM((taps, channels), F32),
            pltpu.VMEM((n // 2, taps, channels), F32),
            dma((4, 3, heads)),
            dma((4, 3, heads)),
            dma((3,)),
            dma((3,)),
            dma((4,)),
            dma((4,)),
            dma((n // 2,)),
            dma((n // 2,)),
            dma((2, heads)),
            dma((5,)),
        ],
        compiler_params=pltpu.CompilerParams(
            collective_id=0, has_side_effects=True, vmem_limit_bytes=62 * 1024 * 1024
        ),
    )(queries, keys, values_in, teacher, gain.reshape(1, channels), conv_weight, block_bits, mask_pos)


def solution(mesh):
    placed = (
        P("tm", "head"),
        P("tm", "head"),
        P("tm", "head"),
        P("tm", "head"),
        P("head"),
        P(None, "head"),
        P("tm", None),
        P("tm", None),
    )
    return jax.shard_map(
        functools.partial(body, mesh.shape["tm"], mesh.shape["head"]),
        mesh=mesh,
        in_specs=placed,
        out_specs=(P("tm", "head"), P("tm", "head"), P("tm", "head"), P(None, "head")),
        check_vma=False,
    )
```

```python
import functools

import jax
import jax.numpy as jnp
from jax import lax
from jax.experimental import pallas as pl
from jax.experimental.pallas import tpu as pltpu
from jax.sharding import PartitionSpec as P

HD = 128
BLK = 128
LOG2E = 1.4426950408889634
NEG_FILL = -1e30
NORM_EPS = 1e-06
MESH = pl.DeviceIdType.MESH
F32 = jnp.float32
BF16 = jnp.bfloat16


def dot_nt(a, b):
    return lax.dot_general(a, b, (((1,), (1,)), ((), ())), preferred_element_type=F32)


def dot_nn(a, b):
    return jnp.dot(a, b, preferred_element_type=F32)


def kernel(
    n,
    width,
    q_hbm,
    k_hbm,
    v_hbm,
    t_hbm,
    gain_hbm,
    w_hbm,
    bits_ref,
    pos_hbm,
    dq_ref,
    dk_ref,
    dv_ref,
    dc_ref,
    v_ref,
    t_ref,
    gain_ref,
    w_ref,
    pos_ref,
    kx,
    vx,
    qx,
    gx,
    stx,
    halo,
    extv,
    dvx,
    prob,
    att,
    mask,
    mask_t,
    stats,
    norm,
    norm_out,
    norm_in,
    tap_pair,
    tap_own,
    tap_all,
    send_sem,
    recv_sem,
    st_send,
    st_recv,
    misc_send,
    misc_recv,
    tap_send,
    tap_recv,
    head_sem,
    in_sem,
):
    rows, channels = q_hbm.shape
    heads = channels // HD
    taps = w_ref.shape[0]
    win = bits_ref.shape[1]
    span = win * BLK
    total = kx.shape[1]
    me = lax.axis_index("tm")
    side = lax.axis_index("head")
    even = lax.rem(me, 2) == 0
    odd = lax.rem(me, 2) == 1
    chips = n // 2
    scale = HD ** (-0.5)
    scale2 = scale * LOG2E

    def cols(h):
        return pl.ds(pl.multiple_of(h * HD, HD), HD)

    def put(buf, lead, src, dst, count, send, recv, target):
        return pltpu.make_async_remote_copy(
            src_ref=buf.at[lead, pl.ds(src, count)],
            dst_ref=buf.at[lead, pl.ds(dst, count)],
            send_sem=send,
            recv_sem=recv,
            device_id={"tm": target},
            device_id_type=MESH,
        )

    own = total - rows

    def ahead_direct(buf, a, h):
        s, r = send_sem.at[a], recv_sem.at[a]
        return [
            (me + 2 < n, put(buf, h, own, BLK, rows, s.at[0, h], r.at[1, h], me + 2)),
            (even, put(buf, h, own, BLK + rows, rows, s.at[1, h], r.at[0, h], me + 1)),
            (
                odd & (me + 3 < n),
                put(buf, h, own + BLK, 0, BLK, s.at[1, h], r.at[2, h], me + 3),
            ),
        ]

    def ahead_relay(buf, a, h):
        s, r = send_sem.at[a], recv_sem.at[a]
        return [
            (odd & (me >= 2), put(buf, h, BLK, BLK + rows, rows, s.at[2, h], r.at[0, h], me - 1)),
            (even & (me >= 2), put(buf, h, BLK + BLK, 0, BLK, s.at[2, h], r.at[2, h], me + 1)),
        ]

    def back_direct(buf, a, h):
        s, r = send_sem.at[a], recv_sem.at[a]
        return [
            (me >= 2, put(buf, h, 0, 2 * rows, rows, s.at[0, h], r.at[1, h], me - 2)),
            (odd, put(buf, h, 0, rows, rows, s.at[1, h], r.at[0, h], me - 1)),
            (
                even & (me >= 3),
                put(buf, h, 0, 3 * rows, BLK, s.at[1, h], r.at[2, h], me - 3),
            ),
        ]

    def back_relay(buf, a, h):
        s, r = send_sem.at[a], recv_sem.at[a]
        return [
            (even & (me + 2 < n), put(buf, h, 2 * rows, rows, rows, s.at[2, h], r.at[0, h], me + 1)),
            (odd & (me + 2 < n), put(buf, h, 2 * rows, 3 * rows, BLK, s.at[2, h], r.at[2, h], me - 1)),
        ]

    def put_stat(src, dst, count, kind, slot, target):
        return pltpu.make_async_remote_copy(
            src_ref=stx.at[:, pl.ds(src, count)],
            dst_ref=stx.at[:, pl.ds(dst, count)],
            send_sem=st_send.at[kind],
            recv_sem=st_recv.at[slot],
            device_id={"tm": target},
            device_id_type=MESH,
        )

    def stat_direct():
        return [
            (me >= 2, put_stat(0, 2 * rows, rows, 0, 1, me - 2)),
            (odd, put_stat(0, rows, rows, 1, 0, me - 1)),
            (even & (me >= 3), put_stat(0, 3 * rows, BLK, 1, 2, me - 3)),
        ]

    def stat_relay():
        return [
            (even & (me + 2 < n), put_stat(2 * rows, rows, rows, 2, 0, me + 1)),
            (odd & (me + 2 < n), put_stat(2 * rows, 3 * rows, BLK, 2, 2, me - 1)),
        ]

    def start(copies):
        for ok, copy in copies:
            pl.when(ok)(copy.start)

    def sent(copies):
        for ok, copy in copies:
            pl.when(ok)(copy.wait_send)

    def got_ahead(buf, a, h, slot):
        dst, count = ((BLK + rows, rows), (BLK, rows), (0, BLK))[slot - 1]
        copy = put(buf, h, dst, dst, count, send_sem.at[a, 0, h], recv_sem.at[a, slot - 1, h], me)
        pl.when(me >= slot)(copy.wait_recv)

    def got_back(buf, a, h, slot):
        dst, count = slot * rows, BLK if slot == 3 else rows
        copy = put(buf, h, dst, dst, count, send_sem.at[a, 0, h], recv_sem.at[a, slot - 1, h], me)
        pl.when(me + slot < n)(copy.wait_recv)

    def got_stat(slot):
        dst, count = slot * rows, BLK if slot == 3 else rows
        pl.when(me + slot < n)(put_stat(dst, dst, count, 0, slot - 1, me).wait_recv)

    def each(body):
        def step(h, carry):
            body(h)
            return carry

        lax.fori_loop(0, heads, step, 0)

    def each_pair(body):
        def step(g, carry):
            body((2 * g, 2 * g + 1))
            return carry

        lax.fori_loop(0, heads // 2, step, 0)

    barrier = pltpu.get_barrier_semaphore()

    def greet(i, carry):
        pl.semaphore_signal(
            barrier, inc=1, device_id={"tm": lax.rem(me + i, n)}, device_id_type=MESH
        )
        return carry

    lax.fori_loop(1, n, greet, 0)
    pl.semaphore_signal(barrier, inc=1, device_id={"head": 1 - side}, device_id_type=MESH)

    halo_rows = halo.shape[0]

    def load_key(h):
        return pltpu.make_async_copy(
            k_hbm.at[:, cols(h)], kx.at[h, pl.ds(own, rows)], head_sem.at[0, h]
        )

    def load_query(h):
        return pltpu.make_async_copy(
            q_hbm.at[:, cols(h)], qx.at[h, pl.ds(0, rows)], head_sem.at[1, h]
        )

    loads = [
        pltpu.make_async_copy(a, b, in_sem.at[i])
        for i, (a, b) in enumerate(
            (
                (v_hbm, v_ref),
                (w_hbm, w_ref),
                (gain_hbm, gain_ref),
                (pos_hbm, pos_ref),
                (t_hbm, t_ref),
            )
        )
    ]
    loads[0].start()
    each(lambda h: load_key(h).start())
    for load in loads[1:]:
        load.start()
    each(lambda h: load_query(h).start())
    loads[0].wait()
    pl.semaphore_wait(barrier, n)

    halo_copy = pltpu.make_async_remote_copy(
        src_ref=v_ref.at[pl.ds(rows - halo_rows, halo_rows)],
        dst_ref=halo,
        send_sem=misc_send.at[0],
        recv_sem=misc_recv.at[0],
        device_id={"tm": me + 1},
        device_id_type=MESH,
    )
    pl.when(me + 1 < n)(halo_copy.start)

    first = heads // 2

    @functools.partial(each)
    def _(h):
        load_key(h).wait()
        pl.when(h < first)(lambda: start(ahead_direct(kx, 0, h)))

    for load in loads[1:]:
        load.wait()

    for slot, (dst, count) in enumerate(((BLK + rows, rows), (BLK, rows), (0, BLK)), 1):

        @pl.when(me < slot)
        def _(dst=dst, count=count):
            @functools.partial(each)
            def _(h):
                kx[h, dst : dst + count, :] = jnp.zeros((count, HD), BF16)
                vx[h, dst : dst + count, :] = jnp.zeros((count, HD), BF16)

        back, back_count = slot * rows, BLK if slot == 3 else rows

        @pl.when(me + slot >= n)
        def _(dst=back, count=back_count):
            @functools.partial(each)
            def _(h):
                qx[h, dst : dst + count, :] = jnp.zeros((count, HD), BF16)
                gx[h, dst : dst + count, :] = jnp.zeros((count, HD), BF16)

            stx[:, dst : dst + count] = jnp.full((stx.shape[0], count), NEG_FILL, F32)

    @pl.when(me < 1)
    def _():
        halo[...] = jnp.zeros(halo.shape, BF16)

    pl.when(me >= 1)(halo_copy.wait_recv)

    @functools.partial(each)
    def _(h):
        extv[h, 0:8, :] = halo[:, cols(h)].astype(F32)[halo_rows - 8 :]
        extv[h, 8 : 8 + rows, :] = v_ref[:, cols(h)].astype(F32)
        acc = jnp.zeros((rows, HD), F32)
        for j in range(taps):
            acc = acc + w_ref[j : j + 1, cols(h)] * extv[h, 8 - j : 8 - j + rows, :]
        vx[h, own:total, :] = acc.astype(BF16)
        start(ahead_direct(vx, 1, h))
        pl.when(h + first < heads)(lambda: start(ahead_direct(kx, 0, h + first)))

    each(lambda h: load_query(h).wait())

    line = lax.broadcasted_iota(jnp.int32, (BLK, BLK), 0)
    lane = lax.broadcasted_iota(jnp.int32, (BLK, BLK), 1)
    for i in range(rows // BLK):
        for r in range(win):
            bit = bits_ref[i, r] > 0
            there = me * (rows // BLK) + i - r >= 0
            part = jnp.full((BLK, BLK), jnp.where(bit & there, 0.0, NEG_FILL), F32)
            if r == 0:
                part = jnp.where(lane <= line, part, NEG_FILL)
            mask[i, :, (win - 1 - r) * BLK : (win - r) * BLK] = part
            stx[3 * heads + r : 3 * heads + r + 1, i * BLK : (i + 1) * BLK] = jnp.full(
                (1, BLK), jnp.where(bit, 0.0, NEG_FILL), F32
            )

    @functools.partial(each)
    def _(h):
        prob[h, 0:BLK, span:total] = jnp.zeros((BLK, total - span), F32)
        prob[h, rows - BLK : rows, 0 : rows - BLK] = jnp.zeros((BLK, rows - BLK), F32)

    stats[...] = jnp.zeros(stats.shape, F32)
    norm[...] = jnp.zeros(norm.shape, F32)

    def relay_kv(h):
        got_ahead(kx, 0, h, 2)
        start(ahead_relay(kx, 0, h))
        got_ahead(vx, 1, h, 2)
        start(ahead_relay(vx, 1, h))

    relay_kv(0)

    @functools.partial(each)
    def _(h):
        pl.when(h + 1 < heads)(lambda: relay_kv(h + 1))
        got_ahead(kx, 0, h, 1)
        got_ahead(kx, 0, h, 3)
        got_ahead(vx, 1, h, 1)
        got_ahead(vx, 1, h, 3)

        @pl.when(h >= first)
        def _():
            start(back_direct(qx, 2, 2 * (h - first)))
            start(back_direct(qx, 2, 2 * (h - first) + 1))

        gain = gain_ref[:, cols(h)]
        for i in range(rows // BLK):
            here = slice(i * BLK, (i + 1) * BLK)
            window = slice(i * BLK, i * BLK + span)
            s = dot_nt(qx[h, here, :], kx[h, window, :]) * scale2 + mask[i]
            peak = jnp.max(s, axis=1, keepdims=True)
            e = jnp.exp2(s - peak)
            inv = 1.0 / jnp.sum(e, axis=1, keepdims=True)
            p = e * inv
            prob[h, here, window] = p
            o = dot_nn(p.astype(BF16), vx[h, window, :])
            att[h, here, :] = o
            stats[here, :] = jnp.where(
                lane == h, -peak, jnp.where(lane == heads + h, inv, stats[here, :])
            )
            og = o * gain
            norm[0, here, :] += o * o
            norm[1, here, :] += og * og
            norm[2, here, :] += og * t_ref[here, cols(h)].astype(F32)

    big_lane = lax.broadcasted_iota(jnp.int32, (rows, HD), 1)
    sums = [jnp.sum(norm[i], axis=1, keepdims=True) for i in range(3)]
    norm_out[...] = jnp.where(
        big_lane == 0, sums[0], jnp.where(big_lane == 1, sums[1], sums[2])
    )
    norm_copy = pltpu.make_async_remote_copy(
        src_ref=norm_out,
        dst_ref=norm_in,
        send_sem=misc_send.at[1],
        recv_sem=misc_recv.at[1],
        device_id={"head": 1 - side},
        device_id_type=MESH,
    )
    norm_copy.start()
    chosen = jnp.concatenate(
        [
            jnp.max(
                jnp.where(
                    pos_ref[i : i + 1, :]
                    == lax.broadcasted_iota(jnp.int32, (BLK, pos_ref.shape[1]), 0),
                    1.0,
                    0.0,
                ),
                axis=1,
                keepdims=True,
            )
            for i in range(rows // BLK)
        ],
        axis=0,
    )
    norm_copy.wait_recv()
    both = norm_out[...] + norm_in[...]
    inverse = lax.rsqrt(both[:, 0:1] / width + NORM_EPS)
    cross = chosen * (inverse * both[:, 1:2] - both[:, 2:3])
    factor = inverse * inverse * inverse * cross / width

    @functools.partial(each)
    def _(h):
        gain = gain_ref[:, cols(h)]
        o = att[h]
        scaled = (o * inverse * gain - t_ref[:, cols(h)].astype(F32)) * chosen * gain
        grad = (inverse * scaled - o * factor).astype(BF16)
        gx[h, 0:rows, :] = grad
        delta = jnp.sum(grad.astype(F32) * o, axis=1, keepdims=True)
        stats[...] = jnp.where(big_lane == 2 * heads + h, delta, stats[...])

    stx[0 : 3 * heads, 0:rows] = stats[...].T[0 : 3 * heads]
    stx[3 * heads + win :, 0:rows] = jnp.zeros((stx.shape[0] - 3 * heads - win, rows), F32)
    start(stat_direct())
    each(lambda h: start(back_direct(gx, 3, h)))

    @functools.partial(each_pair)
    def _(pair):
        for h in pair:
            grad = gx[h, 0:rows, :]
            delta = jnp.sum(grad.astype(F32) * att[h], axis=1, keepdims=True)
            dp = dot_nt(grad, vx[h])
            ds = (prob[h] * (dp - delta)).astype(BF16)
            dq_ref[:, cols(h)] = (dot_nn(ds, kx[h]) * scale).astype(BF16)

    def relay_qg(h):
        got_back(qx, 2, h, 2)
        start(back_relay(qx, 2, h))
        got_back(gx, 3, h, 2)
        start(back_relay(gx, 3, h))

    got_stat(2)
    start(stat_relay())
    relay_qg(0)
    relay_qg(1)
    got_stat(1)
    got_stat(3)
    mask_t[...] = jnp.full(mask_t.shape, NEG_FILL, F32)
    for i in range(rows // BLK):
        for r in range(win):
            part = jnp.broadcast_to(
                stx[3 * heads + r : 3 * heads + r + 1, (i + r) * BLK : (i + r + 1) * BLK],
                (BLK, BLK),
            )
            if r == 0:
                part = jnp.where(line <= lane, part, NEG_FILL)
            mask_t[i * BLK : (i + 1) * BLK, (i + r) * BLK : (i + r + 1) * BLK] = part

    @functools.partial(each_pair)
    def _(pair):
        @pl.when(pair[1] + 1 < heads)
        def _():
            relay_qg(pair[1] + 1)
            relay_qg(pair[1] + 2)

        for h in pair:
            for slot in (1, 3):
                got_back(qx, 2, h, slot)
                got_back(gx, 3, h, slot)
        for h in pair:
            peak = stx[pl.ds(h, 1), :]
            inv = stx[pl.ds(heads + h, 1), :]
            delta = stx[pl.ds(2 * heads + h, 1), :]
            s = dot_nt(kx[h, own:total, :], qx[h]) * scale2 + mask_t[...]
            p = jnp.exp2(s + peak) * inv
            dvx[h, 0:rows, :] = dot_nn(p.astype(BF16), gx[h])
            dp = dot_nt(vx[h, own:total, :], gx[h])
            ds = (p * (dp - delta)).astype(BF16)
            dk_ref[:, cols(h)] = (dot_nn(ds, qx[h]) * scale).astype(BF16)
        for h in pair:
            for j in range(taps):
                tap_own[j : j + 1, cols(h)] = jnp.sum(
                    dvx[h, 0:rows, :] * extv[h, 8 - j : 8 - j + rows, :], axis=0, keepdims=True
                )

    rim_copy = pltpu.make_async_remote_copy(
        src_ref=dvx.at[:, pl.ds(0, 8)],
        dst_ref=dvx.at[:, pl.ds(rows, 8)],
        send_sem=misc_send.at[2],
        recv_sem=misc_recv.at[2],
        device_id={"tm": me - 1},
        device_id_type=MESH,
    )
    pair_copy = pltpu.make_async_remote_copy(
        src_ref=tap_own,
        dst_ref=tap_pair,
        send_sem=misc_send.at[3],
        recv_sem=misc_recv.at[3],
        device_id={"tm": me + 1 - 2 * lax.rem(me, 2)},
        device_id_type=MESH,
    )
    pair_copy.start()
    pl.when(me >= 1)(rim_copy.start)
    core = lax.rem(me, 2)
    chip = me // 2
    pair_copy.wait_recv()
    tap_all[chip] = tap_own[...] + tap_pair[...]

    def share(k):
        return pltpu.make_async_remote_copy(
            src_ref=tap_all.at[chip],
            dst_ref=tap_all.at[chip],
            send_sem=tap_send.at[k],
            recv_sem=tap_recv.at[k],
            device_id={"tm": lax.rem(chip + k, chips) * 2 + core},
            device_id_type=MESH,
        )

    def got_share(k):
        source = lax.rem(chip + chips - k, chips)
        return pltpu.make_async_remote_copy(
            src_ref=tap_all.at[source],
            dst_ref=tap_all.at[source],
            send_sem=tap_send.at[k],
            recv_sem=tap_recv.at[k],
            device_id={"tm": me},
            device_id_type=MESH,
        )

    def run(first, last, body):
        def step(k, carry):
            body(k)
            return carry

        lax.fori_loop(first, last, step, 0)

    run(1, chips, lambda k: share(k).start())

    @pl.when(me + 1 >= n)
    def _():
        dvx[:, rows : rows + 8, :] = jnp.zeros((heads, 8, HD), F32)

    pl.when(me + 1 < n)(rim_copy.wait_recv)

    @functools.partial(each)
    def _(h):
        acc = jnp.zeros((rows, HD), F32)
        for j in range(taps):
            acc = acc + w_ref[j : j + 1, cols(h)] * dvx[h, j : j + rows, :]
        dv_ref[:, cols(h)] = acc.astype(BF16)

    @functools.partial(each)
    def _(h):
        sent(ahead_direct(kx, 0, h))
        sent(ahead_relay(kx, 0, h))
        sent(ahead_direct(vx, 1, h))
        sent(ahead_relay(vx, 1, h))
        sent(back_direct(qx, 2, h))
        sent(back_relay(qx, 2, h))
        sent(back_direct(gx, 3, h))
        sent(back_relay(gx, 3, h))

    sent(stat_direct())
    sent(stat_relay())
    pl.when(me + 1 < n)(halo_copy.wait_send)
    norm_copy.wait_send()
    pl.when(me >= 1)(rim_copy.wait_send)
    pair_copy.wait_send()
    run(1, chips, lambda k: got_share(k).wait_recv())
    acc = tap_all[0]
    for c in range(1, chips):
        acc = acc + tap_all[c]
    dc_ref[...] = acc
    run(1, chips, lambda k: share(k).wait_send())


def body(n, parts, queries, keys, values_in, teacher, gain, conv_weight, block_bits, mask_pos):
    rows, channels = queries.shape
    heads = channels // HD
    taps = conv_weight.shape[0]
    win = block_bits.shape[1]
    span = win * BLK
    total = span + rows - BLK
    blocks = rows // BLK
    stat_rows = -(-(3 * heads + win) // 8) * 8
    vmem = pl.BlockSpec(memory_space=pltpu.VMEM)
    hbm = pl.BlockSpec(memory_space=pl.ANY)
    smem = pl.BlockSpec(memory_space=pltpu.SMEM)
    dma = pltpu.SemaphoreType.DMA
    return pl.pallas_call(
        functools.partial(kernel, n, channels * parts),
        out_shape=(
            jax.ShapeDtypeStruct((rows, channels), BF16),
            jax.ShapeDtypeStruct((rows, channels), BF16),
            jax.ShapeDtypeStruct((rows, channels), BF16),
            jax.ShapeDtypeStruct((taps, channels), F32),
        ),
        in_specs=[hbm] * 6 + [smem, hbm],
        out_specs=(vmem,) * 4,
        scratch_shapes=[
            pltpu.VMEM((rows, channels), BF16),
            pltpu.VMEM((rows, channels), BF16),
            pltpu.VMEM((1, channels), F32),
            pltpu.VMEM((taps, channels), F32),
            pltpu.VMEM(mask_pos.shape, jnp.int32),
            pltpu.VMEM((heads, total, HD), BF16),
            pltpu.VMEM((heads, total, HD), BF16),
            pltpu.VMEM((heads, total, HD), BF16),
            pltpu.VMEM((heads, total, HD), BF16),
            pltpu.VMEM((stat_rows, total), F32),
            pltpu.VMEM((16, channels), BF16),
            pltpu.VMEM((heads, rows + 8, HD), F32),
            pltpu.VMEM((heads, rows + 8, HD), F32),
            pltpu.VMEM((heads, rows, total), F32),
            pltpu.VMEM((heads, rows, HD), F32),
            pltpu.VMEM((blocks, BLK, span), F32),
            pltpu.VMEM((rows, total), F32),
            pltpu.VMEM((rows, HD), F32),
            pltpu.VMEM((3, rows, HD), F32),
            pltpu.VMEM((rows, HD), F32),
            pltpu.VMEM((rows, HD), F32),
            pltpu.VMEM((taps, channels), F32),
            pltpu.VMEM((taps, channels), F32),
            pltpu.VMEM((n // 2, taps, channels), F32),
            dma((4, 3, heads)),
            dma((4, 3, heads)),
            dma((3,)),
            dma((3,)),
            dma((4,)),
            dma((4,)),
            dma((n // 2,)),
            dma((n // 2,)),
            dma((2, heads)),
            dma((5,)),
        ],
        compiler_params=pltpu.CompilerParams(
            collective_id=0, has_side_effects=True, vmem_limit_bytes=62 * 1024 * 1024
        ),
    )(queries, keys, values_in, teacher, gain.reshape(1, channels), conv_weight, block_bits, mask_pos)


def solution(mesh):
    placed = (
        P("tm", "head"),
        P("tm", "head"),
        P("tm", "head"),
        P("tm", "head"),
        P("head"),
        P(None, "head"),
        P("tm", None),
        P("tm", None),
    )
    return jax.shard_map(
        functools.partial(body, mesh.shape["tm"], mesh.shape["head"]),
        mesh=mesh,
        in_specs=placed,
        out_specs=(P("tm", "head"), P("tm", "head"), P("tm", "head"), P(None, "head")),
        check_vma=False,
    )
```

```python
import functools

import jax
import jax.numpy as jnp
from jax import lax
from jax.experimental import pallas as pl
from jax.experimental.pallas import tpu as pltpu
from jax.sharding import PartitionSpec as P

HD = 128
BLK = 128
LOG2E = 1.4426950408889634
NEG_FILL = -1e30
NORM_EPS = 1e-06
MESH = pl.DeviceIdType.MESH
F32 = jnp.float32
BF16 = jnp.bfloat16


def dot_nt(a, b):
    return lax.dot_general(a, b, (((1,), (1,)), ((), ())), preferred_element_type=F32)


def dot_nn(a, b):
    return jnp.dot(a, b, preferred_element_type=F32)


def kernel(
    n,
    width,
    q_hbm,
    k_hbm,
    v_hbm,
    t_hbm,
    gain_hbm,
    w_hbm,
    bits_ref,
    pos_hbm,
    dq_ref,
    dk_ref,
    dv_ref,
    dc_ref,
    v_ref,
    t_ref,
    gain_ref,
    w_ref,
    pos_ref,
    kx,
    vx,
    qx,
    gx,
    stx,
    halo,
    extv,
    dvx,
    prob,
    att,
    mask,
    mask_t,
    stats,
    norm,
    norm_out,
    norm_in,
    tap_pair,
    tap_own,
    tap_all,
    send_sem,
    recv_sem,
    st_send,
    st_recv,
    misc_send,
    misc_recv,
    tap_send,
    tap_recv,
    head_sem,
    in_sem,
):
    rows, channels = q_hbm.shape
    heads = channels // HD
    taps = w_ref.shape[0]
    win = bits_ref.shape[1]
    span = win * BLK
    total = kx.shape[1]
    me = lax.axis_index("tm")
    side = lax.axis_index("head")
    even = lax.rem(me, 2) == 0
    odd = lax.rem(me, 2) == 1
    chips = n // 2
    scale = HD ** (-0.5)
    scale2 = scale * LOG2E

    def cols(h):
        return pl.ds(pl.multiple_of(h * HD, HD), HD)

    def put(buf, lead, src, dst, count, send, recv, target):
        return pltpu.make_async_remote_copy(
            src_ref=buf.at[lead, pl.ds(src, count)],
            dst_ref=buf.at[lead, pl.ds(dst, count)],
            send_sem=send,
            recv_sem=recv,
            device_id={"tm": target},
            device_id_type=MESH,
        )

    own = total - rows

    def ahead_direct(buf, a, h):
        s, r = send_sem.at[a], recv_sem.at[a]
        return [
            (me + 2 < n, put(buf, h, own, BLK, rows, s.at[0, h], r.at[1, h], me + 2)),
            (even, put(buf, h, own, BLK + rows, rows, s.at[1, h], r.at[0, h], me + 1)),
            (
                odd & (me + 3 < n),
                put(buf, h, own + BLK, 0, BLK, s.at[1, h], r.at[2, h], me + 3),
            ),
        ]

    def ahead_relay(buf, a, h):
        s, r = send_sem.at[a], recv_sem.at[a]
        return [
            (odd & (me >= 2), put(buf, h, BLK, BLK + rows, rows, s.at[2, h], r.at[0, h], me - 1)),
            (even & (me >= 2), put(buf, h, BLK + BLK, 0, BLK, s.at[2, h], r.at[2, h], me + 1)),
        ]

    def back_direct(buf, a, h):
        s, r = send_sem.at[a], recv_sem.at[a]
        return [
            (me >= 2, put(buf, h, 0, 2 * rows, rows, s.at[0, h], r.at[1, h], me - 2)),
            (odd, put(buf, h, 0, rows, rows, s.at[1, h], r.at[0, h], me - 1)),
            (
                even & (me >= 3),
                put(buf, h, 0, 3 * rows, BLK, s.at[1, h], r.at[2, h], me - 3),
            ),
        ]

    def back_relay(buf, a, h):
        s, r = send_sem.at[a], recv_sem.at[a]
        return [
            (even & (me + 2 < n), put(buf, h, 2 * rows, rows, rows, s.at[2, h], r.at[0, h], me + 1)),
            (odd & (me + 2 < n), put(buf, h, 2 * rows, 3 * rows, BLK, s.at[2, h], r.at[2, h], me - 1)),
        ]

    def put_stat(src, dst, count, kind, slot, target):
        return pltpu.make_async_remote_copy(
            src_ref=stx.at[:, pl.ds(src, count)],
            dst_ref=stx.at[:, pl.ds(dst, count)],
            send_sem=st_send.at[kind],
            recv_sem=st_recv.at[slot],
            device_id={"tm": target},
            device_id_type=MESH,
        )

    def stat_direct():
        return [
            (me >= 2, put_stat(0, 2 * rows, rows, 0, 1, me - 2)),
            (odd, put_stat(0, rows, rows, 1, 0, me - 1)),
            (even & (me >= 3), put_stat(0, 3 * rows, BLK, 1, 2, me - 3)),
        ]

    def stat_relay():
        return [
            (even & (me + 2 < n), put_stat(2 * rows, rows, rows, 2, 0, me + 1)),
            (odd & (me + 2 < n), put_stat(2 * rows, 3 * rows, BLK, 2, 2, me - 1)),
        ]

    def start(copies):
        for ok, copy in copies:
            pl.when(ok)(copy.start)

    def sent(copies):
        for ok, copy in copies:
            pl.when(ok)(copy.wait_send)

    def got_ahead(buf, a, h, slot):
        dst, count = ((BLK + rows, rows), (BLK, rows), (0, BLK))[slot - 1]
        copy = put(buf, h, dst, dst, count, send_sem.at[a, 0, h], recv_sem.at[a, slot - 1, h], me)
        pl.when(me >= slot)(copy.wait_recv)

    def got_back(buf, a, h, slot):
        dst, count = slot * rows, BLK if slot == 3 else rows
        copy = put(buf, h, dst, dst, count, send_sem.at[a, 0, h], recv_sem.at[a, slot - 1, h], me)
        pl.when(me + slot < n)(copy.wait_recv)

    def got_stat(slot):
        dst, count = slot * rows, BLK if slot == 3 else rows
        pl.when(me + slot < n)(put_stat(dst, dst, count, 0, slot - 1, me).wait_recv)

    def each(body):
        def step(h, carry):
            body(h)
            return carry

        lax.fori_loop(0, heads, step, 0)

    barrier = pltpu.get_barrier_semaphore()

    def greet(i, carry):
        pl.semaphore_signal(
            barrier, inc=1, device_id={"tm": lax.rem(me + i, n)}, device_id_type=MESH
        )
        return carry

    lax.fori_loop(1, n, greet, 0)
    pl.semaphore_signal(barrier, inc=1, device_id={"head": 1 - side}, device_id_type=MESH)

    halo_rows = halo.shape[0]

    def load_key(h):
        return pltpu.make_async_copy(
            k_hbm.at[:, cols(h)], kx.at[h, pl.ds(own, rows)], head_sem.at[0, h]
        )

    def load_query(h):
        return pltpu.make_async_copy(
            q_hbm.at[:, cols(h)], qx.at[h, pl.ds(0, rows)], head_sem.at[1, h]
        )

    loads = [
        pltpu.make_async_copy(a, b, in_sem.at[i])
        for i, (a, b) in enumerate(
            (
                (v_hbm, v_ref),
                (w_hbm, w_ref),
                (gain_hbm, gain_ref),
                (pos_hbm, pos_ref),
                (t_hbm, t_ref),
            )
        )
    ]
    loads[0].start()
    each(lambda h: load_key(h).start())
    for load in loads[1:]:
        load.start()
    each(lambda h: load_query(h).start())
    loads[0].wait()
    pl.semaphore_wait(barrier, n)

    halo_copy = pltpu.make_async_remote_copy(
        src_ref=v_ref.at[pl.ds(rows - halo_rows, halo_rows)],
        dst_ref=halo,
        send_sem=misc_send.at[0],
        recv_sem=misc_recv.at[0],
        device_id={"tm": me + 1},
        device_id_type=MESH,
    )
    pl.when(me + 1 < n)(halo_copy.start)

    first = heads // 2

    @functools.partial(each)
    def _(h):
        load_key(h).wait()
        pl.when(h < first)(lambda: start(ahead_direct(kx, 0, h)))

    for load in loads[1:]:
        load.wait()

    for slot, (dst, count) in enumerate(((BLK + rows, rows), (BLK, rows), (0, BLK)), 1):

        @pl.when(me < slot)
        def _(dst=dst, count=count):
            @functools.partial(each)
            def _(h):
                kx[h, dst : dst + count, :] = jnp.zeros((count, HD), BF16)
                vx[h, dst : dst + count, :] = jnp.zeros((count, HD), BF16)

        back, back_count = slot * rows, BLK if slot == 3 else rows

        @pl.when(me + slot >= n)
        def _(dst=back, count=back_count):
            @functools.partial(each)
            def _(h):
                qx[h, dst : dst + count, :] = jnp.zeros((count, HD), BF16)
                gx[h, dst : dst + count, :] = jnp.zeros((count, HD), BF16)

            stx[:, dst : dst + count] = jnp.full((stx.shape[0], count), NEG_FILL, F32)

    @pl.when(me < 1)
    def _():
        halo[...] = jnp.zeros(halo.shape, BF16)

    pl.when(me >= 1)(halo_copy.wait_recv)

    @functools.partial(each)
    def _(h):
        extv[h, 0:8, :] = halo[:, cols(h)].astype(F32)[halo_rows - 8 :]
        extv[h, 8 : 8 + rows, :] = v_ref[:, cols(h)].astype(F32)
        acc = jnp.zeros((rows, HD), F32)
        for j in range(taps):
            acc = acc + w_ref[j : j + 1, cols(h)] * extv[h, 8 - j : 8 - j + rows, :]
        vx[h, own:total, :] = acc.astype(BF16)
        start(ahead_direct(vx, 1, h))
        pl.when(h + first < heads)(lambda: start(ahead_direct(kx, 0, h + first)))

    each(lambda h: load_query(h).wait())

    line = lax.broadcasted_iota(jnp.int32, (BLK, BLK), 0)
    lane = lax.broadcasted_iota(jnp.int32, (BLK, BLK), 1)
    for i in range(rows // BLK):
        for r in range(win):
            bit = bits_ref[i, r] > 0
            there = me * (rows // BLK) + i - r >= 0
            part = jnp.full((BLK, BLK), jnp.where(bit & there, 0.0, NEG_FILL), F32)
            if r == 0:
                part = jnp.where(lane <= line, part, NEG_FILL)
            mask[i, :, (win - 1 - r) * BLK : (win - r) * BLK] = part
            stx[3 * heads + r : 3 * heads + r + 1, i * BLK : (i + 1) * BLK] = jnp.full(
                (1, BLK), jnp.where(bit, 0.0, NEG_FILL), F32
            )

    stats[...] = jnp.zeros(stats.shape, F32)
    norm[...] = jnp.zeros(norm.shape, F32)

    def relay_kv(h):
        got_ahead(kx, 0, h, 2)
        start(ahead_relay(kx, 0, h))
        got_ahead(vx, 1, h, 2)
        start(ahead_relay(vx, 1, h))

    relay_kv(0)

    @functools.partial(each)
    def _(h):
        pl.when(h + 1 < heads)(lambda: relay_kv(h + 1))
        got_ahead(kx, 0, h, 1)
        got_ahead(kx, 0, h, 3)
        got_ahead(vx, 1, h, 1)
        got_ahead(vx, 1, h, 3)

        start(back_direct(qx, 2, h))
        gain = gain_ref[:, cols(h)]
        for i in range(rows // BLK):
            here = slice(i * BLK, (i + 1) * BLK)
            window = slice(i * BLK, i * BLK + span)
            s = dot_nt(qx[h, here, :], kx[h, window, :]) * scale2 + mask[i]
            peak = jnp.max(s, axis=1, keepdims=True)
            e = jnp.exp2(s - peak)
            inv = 1.0 / jnp.sum(e, axis=1, keepdims=True)
            p = e * inv
            prob[h, i] = p
            o = dot_nn(p.astype(BF16), vx[h, window, :])
            att[h, here, :] = o
            stats[here, :] = jnp.where(
                lane == h, -peak, jnp.where(lane == heads + h, inv, stats[here, :])
            )
            og = o * gain
            norm[0, here, :] += o * o
            norm[1, here, :] += og * og
            norm[2, here, :] += og * t_ref[here, cols(h)].astype(F32)

    big_lane = lax.broadcasted_iota(jnp.int32, (rows, HD), 1)
    sums = [jnp.sum(norm[i], axis=1, keepdims=True) for i in range(3)]
    norm_out[...] = jnp.where(
        big_lane == 0, sums[0], jnp.where(big_lane == 1, sums[1], sums[2])
    )
    norm_copy = pltpu.make_async_remote_copy(
        src_ref=norm_out,
        dst_ref=norm_in,
        send_sem=misc_send.at[1],
        recv_sem=misc_recv.at[1],
        device_id={"head": 1 - side},
        device_id_type=MESH,
    )
    norm_copy.start()
    chosen = jnp.concatenate(
        [
            jnp.max(
                jnp.where(
                    pos_ref[i : i + 1, :]
                    == lax.broadcasted_iota(jnp.int32, (BLK, pos_ref.shape[1]), 0),
                    1.0,
                    0.0,
                ),
                axis=1,
                keepdims=True,
            )
            for i in range(rows // BLK)
        ],
        axis=0,
    )
    norm_copy.wait_recv()
    both = norm_out[...] + norm_in[...]
    inverse = lax.rsqrt(both[:, 0:1] / width + NORM_EPS)
    cross = chosen * (inverse * both[:, 1:2] - both[:, 2:3])
    factor = inverse * inverse * inverse * cross / width

    @functools.partial(each)
    def _(h):
        gain = gain_ref[:, cols(h)]
        o = att[h]
        scaled = (o * inverse * gain - t_ref[:, cols(h)].astype(F32)) * chosen * gain
        grad = (inverse * scaled - o * factor).astype(BF16)
        gx[h, 0:rows, :] = grad
        delta = jnp.sum(grad.astype(F32) * o, axis=1, keepdims=True)
        stats[...] = jnp.where(big_lane == 2 * heads + h, delta, stats[...])

    stx[0 : 3 * heads, 0:rows] = stats[...].T[0 : 3 * heads]
    stx[3 * heads + win :, 0:rows] = jnp.zeros((stx.shape[0] - 3 * heads - win, rows), F32)
    start(stat_direct())
    each(lambda h: start(back_direct(gx, 3, h)))

    @functools.partial(each)
    def _(h):
        for i in range(rows // BLK):
            here = slice(i * BLK, (i + 1) * BLK)
            window = slice(i * BLK, i * BLK + span)
            grad = gx[h, here, :]
            delta = jnp.sum(grad.astype(F32) * att[h, here, :], axis=1, keepdims=True)
            dp = dot_nt(grad, vx[h, window, :])
            ds = (prob[h, i] * (dp - delta)).astype(BF16)
            dq_ref[here, cols(h)] = (dot_nn(ds, kx[h, window, :]) * scale).astype(BF16)

    def relay_qg(h):
        got_back(qx, 2, h, 2)
        start(back_relay(qx, 2, h))
        got_back(gx, 3, h, 2)
        start(back_relay(gx, 3, h))

    got_stat(2)
    start(stat_relay())
    relay_qg(0)
    got_stat(1)
    got_stat(3)
    for i in range(rows // BLK):
        for r in range(win):
            part = jnp.broadcast_to(
                stx[3 * heads + r : 3 * heads + r + 1, (i + r) * BLK : (i + r + 1) * BLK],
                (BLK, BLK),
            )
            if r == 0:
                part = jnp.where(line <= lane, part, NEG_FILL)
            mask_t[i, :, r * BLK : (r + 1) * BLK] = part

    @functools.partial(each)
    def _(h):
        pl.when(h + 1 < heads)(lambda: relay_qg(h + 1))
        got_back(qx, 2, h, 1)
        got_back(qx, 2, h, 3)
        got_back(gx, 3, h, 1)
        got_back(gx, 3, h, 3)
        for i in range(rows // BLK):
            here = slice(own + i * BLK, own + (i + 1) * BLK)
            out = slice(i * BLK, (i + 1) * BLK)
            window = slice(i * BLK, i * BLK + span)
            peak = stx[pl.ds(h, 1), window]
            inv = stx[pl.ds(heads + h, 1), window]
            delta = stx[pl.ds(2 * heads + h, 1), window]
            s = dot_nt(kx[h, here, :], qx[h, window, :]) * scale2 + mask_t[i]
            p = jnp.exp2(s + peak) * inv
            dvx[h, out, :] = dot_nn(p.astype(BF16), gx[h, window, :])
            dp = dot_nt(vx[h, here, :], gx[h, window, :])
            ds = (p * (dp - delta)).astype(BF16)
            dk_ref[out, cols(h)] = (dot_nn(ds, qx[h, window, :]) * scale).astype(BF16)
        for j in range(taps):
            tap_own[j : j + 1, cols(h)] = jnp.sum(
                dvx[h, 0:rows, :] * extv[h, 8 - j : 8 - j + rows, :], axis=0, keepdims=True
            )

    rim_copy = pltpu.make_async_remote_copy(
        src_ref=dvx.at[:, pl.ds(0, 8)],
        dst_ref=dvx.at[:, pl.ds(rows, 8)],
        send_sem=misc_send.at[2],
        recv_sem=misc_recv.at[2],
        device_id={"tm": me - 1},
        device_id_type=MESH,
    )
    pair_copy = pltpu.make_async_remote_copy(
        src_ref=tap_own,
        dst_ref=tap_pair,
        send_sem=misc_send.at[3],
        recv_sem=misc_recv.at[3],
        device_id={"tm": me + 1 - 2 * lax.rem(me, 2)},
        device_id_type=MESH,
    )
    pair_copy.start()
    pl.when(me >= 1)(rim_copy.start)
    core = lax.rem(me, 2)
    chip = me // 2
    pair_copy.wait_recv()
    tap_all[chip] = tap_own[...] + tap_pair[...]

    def share(k):
        return pltpu.make_async_remote_copy(
            src_ref=tap_all.at[chip],
            dst_ref=tap_all.at[chip],
            send_sem=tap_send.at[k],
            recv_sem=tap_recv.at[k],
            device_id={"tm": lax.rem(chip + k, chips) * 2 + core},
            device_id_type=MESH,
        )

    def got_share(k):
        source = lax.rem(chip + chips - k, chips)
        return pltpu.make_async_remote_copy(
            src_ref=tap_all.at[source],
            dst_ref=tap_all.at[source],
            send_sem=tap_send.at[k],
            recv_sem=tap_recv.at[k],
            device_id={"tm": me},
            device_id_type=MESH,
        )

    def run(first, last, body):
        def step(k, carry):
            body(k)
            return carry

        lax.fori_loop(first, last, step, 0)

    run(1, chips, lambda k: share(k).start())

    @pl.when(me + 1 >= n)
    def _():
        dvx[:, rows : rows + 8, :] = jnp.zeros((heads, 8, HD), F32)

    pl.when(me + 1 < n)(rim_copy.wait_recv)

    @functools.partial(each)
    def _(h):
        acc = jnp.zeros((rows, HD), F32)
        for j in range(taps):
            acc = acc + w_ref[j : j + 1, cols(h)] * dvx[h, j : j + rows, :]
        dv_ref[:, cols(h)] = acc.astype(BF16)

    @functools.partial(each)
    def _(h):
        sent(ahead_direct(kx, 0, h))
        sent(ahead_relay(kx, 0, h))
        sent(ahead_direct(vx, 1, h))
        sent(ahead_relay(vx, 1, h))
        sent(back_direct(qx, 2, h))
        sent(back_relay(qx, 2, h))
        sent(back_direct(gx, 3, h))
        sent(back_relay(gx, 3, h))

    sent(stat_direct())
    sent(stat_relay())
    pl.when(me + 1 < n)(halo_copy.wait_send)
    norm_copy.wait_send()
    pl.when(me >= 1)(rim_copy.wait_send)
    pair_copy.wait_send()
    run(1, chips, lambda k: got_share(k).wait_recv())
    acc = tap_all[0]
    for c in range(1, chips):
        acc = acc + tap_all[c]
    dc_ref[...] = acc
    run(1, chips, lambda k: share(k).wait_send())


def body(n, parts, queries, keys, values_in, teacher, gain, conv_weight, block_bits, mask_pos):
    rows, channels = queries.shape
    heads = channels // HD
    taps = conv_weight.shape[0]
    win = block_bits.shape[1]
    span = win * BLK
    total = span + rows - BLK
    blocks = rows // BLK
    stat_rows = -(-(3 * heads + win) // 8) * 8
    vmem = pl.BlockSpec(memory_space=pltpu.VMEM)
    hbm = pl.BlockSpec(memory_space=pl.ANY)
    smem = pl.BlockSpec(memory_space=pltpu.SMEM)
    dma = pltpu.SemaphoreType.DMA
    return pl.pallas_call(
        functools.partial(kernel, n, channels * parts),
        out_shape=(
            jax.ShapeDtypeStruct((rows, channels), BF16),
            jax.ShapeDtypeStruct((rows, channels), BF16),
            jax.ShapeDtypeStruct((rows, channels), BF16),
            jax.ShapeDtypeStruct((taps, channels), F32),
        ),
        in_specs=[hbm] * 6 + [smem, hbm],
        out_specs=(vmem,) * 4,
        scratch_shapes=[
            pltpu.VMEM((rows, channels), BF16),
            pltpu.VMEM((rows, channels), BF16),
            pltpu.VMEM((1, channels), F32),
            pltpu.VMEM((taps, channels), F32),
            pltpu.VMEM(mask_pos.shape, jnp.int32),
            pltpu.VMEM((heads, total, HD), BF16),
            pltpu.VMEM((heads, total, HD), BF16),
            pltpu.VMEM((heads, total, HD), BF16),
            pltpu.VMEM((heads, total, HD), BF16),
            pltpu.VMEM((stat_rows, total), F32),
            pltpu.VMEM((16, channels), BF16),
            pltpu.VMEM((heads, rows + 8, HD), F32),
            pltpu.VMEM((heads, rows + 8, HD), F32),
            pltpu.VMEM((heads, blocks, BLK, span), F32),
            pltpu.VMEM((heads, rows, HD), F32),
            pltpu.VMEM((blocks, BLK, span), F32),
            pltpu.VMEM((blocks, BLK, span), F32),
            pltpu.VMEM((rows, HD), F32),
            pltpu.VMEM((3, rows, HD), F32),
            pltpu.VMEM((rows, HD), F32),
            pltpu.VMEM((rows, HD), F32),
            pltpu.VMEM((taps, channels), F32),
            pltpu.VMEM((taps, channels), F32),
            pltpu.VMEM((n // 2, taps, channels), F32),
            dma((4, 3, heads)),
            dma((4, 3, heads)),
            dma((3,)),
            dma((3,)),
            dma((4,)),
            dma((4,)),
            dma((n // 2,)),
            dma((n // 2,)),
            dma((2, heads)),
            dma((5,)),
        ],
        compiler_params=pltpu.CompilerParams(
            collective_id=0, has_side_effects=True, vmem_limit_bytes=62 * 1024 * 1024
        ),
    )(queries, keys, values_in, teacher, gain.reshape(1, channels), conv_weight, block_bits, mask_pos)


def solution(mesh):
    placed = (
        P("tm", "head"),
        P("tm", "head"),
        P("tm", "head"),
        P("tm", "head"),
        P("head"),
        P(None, "head"),
        P("tm", None),
        P("tm", None),
    )
    return jax.shard_map(
        functools.partial(body, mesh.shape["tm"], mesh.shape["head"]),
        mesh=mesh,
        in_specs=placed,
        out_specs=(P("tm", "head"), P("tm", "head"), P("tm", "head"), P(None, "head")),
        check_vma=False,
    )
```
